128 devices in a mesh: row: 8 (over y_hi, x), feat: 16 (over y_lo, z, core).
Axes of the slice: x: 4, y: 4 (y_hi: 2, y_lo: 2; y = y_hi * 2 + y_lo), z: 4, core: 2. Of those that a mesh axis runs over, the one named last changes fastest.
Arguments:
- design_tiles: bfloat16 [8, 8, 8, 48, 128, 128], P('row', None, None, 'feat'), may hold values from -0.078125 to 0.078125
- block_ids: int32 [8, 8, 8, 48], P(None, None, None, 'feat'), may hold values from 0 to 1023, as said below
- responses: bfloat16 [8, 8, 8, 128, 64], P('row'), may hold values from -6 to 6
- live_groups: int32 [8, 8], replicated, may hold values from 0 to 1, as said below
- start_coef: float32 [131072, 64], P('feat'), may hold values from -6 to 6
Outputs:
- coefficients: float32 [131072, 64], P('feat')
The draws below stay inside these ranges and needn't reach their ends.
Inputs may be any that keep to these rules, and one draw needn't show every extreme that they name: `block_ids`: the 3 entries of a row block that lie in feat index f's positions are distinct feature blocks of the range f * 64 to (f + 1) * 64 - 1. `live_groups`: A group is all live or all empty; every owner has live groups from exactly half of the 8 sources.
All inputs are finite; a program needn't handle non-finite values.
Results may differ from the reference program's by a relative error of at most 0.002.
Values may be sent and summed in bfloat16 or wider, within the bound.
No kernel may reach another device: no remote copies, remote signals or barrier semaphores. Data moves between devices by JAX's collectives and lax.ppermute only.
A program may use at most 64 MiB of HBM per device.

```python
import jax
import jax.numpy as jnp
from jax import lax

F = 131072
C = 64
BW = 128
RB = 128
KT = 3
CAP = 8
ITERS = 2
OWNERS = 8
TILES_RB = 48
N_ROW = 8
N_FEAT = 16


def draw_block_ids(key, part):
    local_blocks = F // (BW * N_FEAT)
    scores = jax.random.randint(key, (N_ROW, N_ROW, CAP, N_FEAT, local_blocks), 0, 1 << 20)
    distinct = scores * local_blocks + jnp.arange(local_blocks, dtype=jnp.int32)
    top_values, picks = lax.top_k(distinct, KT)
    shard_base = jnp.arange(N_FEAT, dtype=jnp.int32)[:, None] * local_blocks
    chosen = picks.astype(jnp.int32) + shard_base
    return chosen.reshape(N_ROW, N_ROW, CAP, N_FEAT * KT).astype(jnp.int32)


def draw_live_groups(key, part):
    key_bias = jax.random.fold_in(key, 11)
    key_noise = jax.random.fold_in(key, 23)
    bias = jax.random.randint(key_bias, (N_ROW, 1), 0, 3) * N_ROW
    noise = jax.random.randint(key_noise, (N_ROW, N_ROW), 0, N_ROW)
    score = (bias + noise) * N_ROW + jnp.arange(N_ROW, dtype=jnp.int32)[:, None]
    ranking = jnp.argsort(jnp.argsort(-score, axis=0), axis=0)
    return (ranking < N_ROW // 2).astype(jnp.int32)


def level_of(stream_key, shape, cuts, low, top_value):
    level, own = 1.0, jax.random.fold_in(stream_key, 6)
    for position, parts in cuts:
        heights = jnp.exp(jax.random.uniform(jax.random.fold_in(own, position), (parts,), jnp.float32, low / len(cuts), top_value / len(cuts)))
        level = level * jnp.repeat(heights, shape[position] // parts).reshape([-1 if axis == position else 1 for axis in range(len(shape))])
    return level


def gaussian(rng, extent, spread, most, split=(), kind=jnp.bfloat16):
    drawn = jax.random.normal(rng, extent, jnp.float32) * spread
    if len(split) > 0:
        drawn = level_of(rng, extent, split, -0.22, 0.18) * drawn
    return jnp.clip(drawn, min=-most, max=most).astype(kind)


def setup_inputs(seed: int = 0) -> dict:
    arg_keys = jax.random.split(jax.random.key(seed), 6)
    design_tiles = gaussian(arg_keys[0], (OWNERS, OWNERS, CAP, TILES_RB, RB, BW), (KT * N_FEAT * BW) ** -0.5, 0.078125, ((0, 8), (3, 16)))
    block_ids = draw_block_ids(jax.random.fold_in(arg_keys[5], 71), 0)
    responses = gaussian(arg_keys[2], (OWNERS, OWNERS, CAP, RB, C), 1.0, 6.0, ((0, 8),))
    live_groups = draw_live_groups(jax.random.fold_in(arg_keys[5], 71), 0)
    start_coef = gaussian(arg_keys[4], (F, C), 1.0, 6.0, ((0, 16),), jnp.float32)
    return {"design_tiles": design_tiles, "block_ids": block_ids, "responses": responses, "live_groups": live_groups, "start_coef": start_coef}


step_size = 0.25
ridge_term = 0.05

def reference(design_tiles, block_ids, responses, live_groups, start_coef):
    sources, owners, slot_count, tile_count, block_rows, block_width = design_tiles.shape
    columns = responses.shape[-1]
    all_blocks = start_coef.shape[0] // block_width
    threshold = 1.4 * columns ** 0.5
    pairs = sources * owners
    tile_groups = design_tiles.reshape(pairs, slot_count, tile_count, block_rows, block_width)
    id_groups = block_ids.reshape(pairs, slot_count, tile_count)
    resp_groups = responses.reshape(pairs, slot_count, block_rows, columns)
    flag_groups = live_groups.reshape(pairs).astype(jnp.float32)
    coefficients = start_coef
    for iteration in range(ITERS):
        coef_bf = coefficients.astype(jnp.bfloat16).reshape(all_blocks, block_width, columns)

        def visit(carry, item):
            gradient, curvature = carry
            tiles_now, ids_now, resp_now, flag_now = item
            tiles_wide = tiles_now.astype(jnp.float32)
            picked = coef_bf[ids_now].astype(jnp.float32)
            predicted = jnp.einsum('skif,skfc->sic', tiles_wide, picked, precision=lax.Precision.HIGHEST)
            residual = resp_now.astype(jnp.float32) - predicted
            row_norms = jnp.sqrt(lax.optimization_barrier(jnp.sum(residual * residual, axis=-1)))
            weight = flag_now * threshold / jnp.maximum(row_norms, threshold)
            scaled = (weight[..., None] * residual).astype(jnp.bfloat16)
            rounded = weight.astype(jnp.bfloat16)
            partial_grad = jnp.einsum('skif,sic->skfc', tiles_wide, scaled.astype(jnp.float32), precision=lax.Precision.HIGHEST)
            partial_curv = jnp.einsum('skif,si->skf', tiles_wide * tiles_wide, rounded.astype(jnp.float32), precision=lax.Precision.HIGHEST)
            flat_ids = ids_now.reshape(-1).astype(jnp.int32)
            gradient = gradient + jax.ops.segment_sum(partial_grad.reshape(-1, block_width, columns), flat_ids, num_segments=all_blocks)
            curvature = curvature + jax.ops.segment_sum(partial_curv.reshape(-1, block_width), flat_ids, num_segments=all_blocks)
            return ((gradient, curvature), None)
        empty = (jnp.zeros((all_blocks, block_width, columns), jnp.float32), jnp.zeros((all_blocks, block_width), jnp.float32))
        (gradient, curvature), unused = lax.scan(visit, empty, (tile_groups, id_groups, resp_groups, flag_groups))
        coefficients = coefficients + step_size * (gradient.reshape(-1, columns) - ridge_term * coefficients) / (curvature.reshape(-1, 1) + ridge_term)
    return coefficients
```

```python
import jax
import jax.numpy as jnp
from jax import lax
from jax.experimental import pallas as pl
from jax.experimental.pallas import tpu as pltpu
from jax.sharding import PartitionSpec as P

ITERS = 2
STEP_SIZE = 0.25
RIDGE = 0.05
F32 = jnp.float32
BF16 = jnp.bfloat16
VMEM_LIMIT = 48 * 1024 * 1024

LANES = 128
PAD = 16


def params():
    return pltpu.CompilerParams(vmem_limit_bytes=VMEM_LIMIT)


def coef_blocks(start_t):
    columns, features = start_t.shape
    blocks = features // LANES
    step = 16

    def kernel(start_ref, out_ref):
        for b in range(step):
            out_ref[b] = start_ref[:, b * LANES : (b + 1) * LANES].astype(BF16)

    return pl.pallas_call(
        kernel,
        grid=(blocks // step,),
        in_specs=[pl.BlockSpec((columns, step * LANES), lambda i: (0, i))],
        out_specs=pl.BlockSpec((step, columns, LANES), lambda i: (i, 0, 0)),
        out_shape=jax.ShapeDtypeStruct((blocks, columns, LANES), BF16),
        compiler_params=params(),
    )(start_t)


def predict_half(scalars, ids, tiles, coef, dtype):
    row_blocks, kt, rows, width = tiles.shape
    columns = coef.shape[1]
    half = row_blocks // 2
    step = 8
    steps = half // step

    def kernel(scalars_ref, ids_ref, tiles_ref, coef_ref, out_ref):
        base = (scalars_ref[0] * steps + pl.program_id(0)) * step
        for r in range(step):
            total = None
            for k in range(kt):
                block = ids_ref[(base + r) * kt + k]
                part = lax.dot_general(
                    coef_ref[block],
                    tiles_ref[r, k],
                    (((1,), (1,)), ((), ())),
                    preferred_element_type=F32,
                )
                total = part if total is None else total + part
            out_ref[r] = total.astype(dtype)

    return pl.pallas_call(
        kernel,
        grid_spec=pltpu.PrefetchScalarGridSpec(
            num_scalar_prefetch=2,
            grid=(steps,),
            in_specs=[
                pl.BlockSpec((step, kt, rows, width), lambda i, s, d: (s[0] * steps + i, 0, 0, 0)),
                pl.BlockSpec(coef.shape, lambda i, s, d: (0, 0, 0)),
            ],
            out_specs=pl.BlockSpec((step, columns, rows), lambda i, s, d: (i, 0, 0)),
        ),
        out_shape=jax.ShapeDtypeStruct((half, columns, rows), dtype),
        compiler_params=params(),
    )(scalars, ids, tiles, coef)


def weigh(scalars, parts, resp_t, copies):
    sources, count, columns, rows = parts.shape
    threshold = 1.4 * columns**0.5

    def kernel(scalars_ref, parts_ref, resp_ref, out_ref):
        flag = scalars_ref[1].astype(F32)
        lines = []
        for r in range(count):
            predicted = parts_ref[0, r].astype(F32)
            for s in range(1, sources):
                predicted = predicted + parts_ref[s, r].astype(F32)
            residual = resp_ref[r].astype(F32) - predicted
            norm = jnp.sqrt(jnp.sum(residual * residual, axis=0, keepdims=True))
            weight = flag * threshold / jnp.maximum(norm, threshold)
            scaled = (weight * residual).astype(BF16)
            for c in range(copies):
                out_ref[c, r * columns : (r + 1) * columns, :] = scaled
            lines.append(weight)
        lines.append(jnp.zeros((PAD - count, rows), F32))
        tail = jnp.concatenate(lines, axis=0).astype(BF16)
        for c in range(copies):
            out_ref[c, count * columns :, :] = tail

    height = count * columns + PAD
    return pl.pallas_call(
        kernel,
        grid_spec=pltpu.PrefetchScalarGridSpec(
            num_scalar_prefetch=1,
            grid=(1,),
            in_specs=[
                pl.BlockSpec(parts.shape, lambda i, s: (0, 0, 0, 0)),
                pl.BlockSpec((count, columns, rows), lambda i, s: (s[2], 0, 0)),
            ],
            out_specs=pl.BlockSpec((copies, height, rows), lambda i, s: (0, 0, 0)),
        ),
        out_shape=jax.ShapeDtypeStruct((copies, height, rows), BF16),
        compiler_params=params(),
    )(scalars, parts, resp_t)


def gradient_half(scalars, ids, tiles, scaled, local_blocks, groups, carried=None, before=None, keep_error=False):
    row_blocks, kt, rows, width = tiles.shape
    sources, height, _ = scaled.shape
    count = row_blocks // 2 // sources
    columns = (height - PAD) // count
    per_step = 2
    step = count * per_step
    steps = sources // per_step
    last = before is not None
    owned = local_blocks // groups

    def kernel(scalars_ref, ids_ref, tiles_ref, scaled_ref, *refs):
        refs = list(refs)
        start_ref = refs.pop(0) if last or carried is not None else None
        curv_in = refs.pop(0) if last else None
        if last:
            out_ref = refs.pop(0)
            error_ref = refs.pop(0) if keep_error else None
        grad, curv = refs
        place = pl.program_id(0)
        base = (scalars_ref[0] * steps + place) * step

        @pl.when(place == 0)
        def _():
            if start_ref is not None:
                grad[...] = start_ref[...]
            else:
                grad[...] = jnp.zeros_like(grad)
            if last:
                curv[...] = curv_in[...]
            else:
                curv[...] = jnp.zeros_like(curv)

        for p in range(per_step):
            tail = scaled_ref[p, count * columns :, :].astype(F32)
            for r in range(count):
                weights = jnp.broadcast_to(tail[r : r + 1, :], (rows, rows)).T
                lhs = scaled_ref[p, r * columns : (r + 1) * columns, :]
                at = p * count + r
                for k in range(kt):
                    block = ids_ref[(base + at) * kt + k]
                    tile = tiles_ref[at, k]
                    grad[block] += jnp.dot(lhs, tile, preferred_element_type=F32)
                    wide = tile.astype(F32)
                    square = wide * wide * weights
                    curv[block] += jnp.sum(square.reshape(rows // 8, 8, width), axis=0)

        if last:

            @pl.when(place == steps - 1)
            def _():
                for g in range(groups):
                    lines = []
                    for b in range(owned):
                        at = g * owned + b
                        rounded = grad[at].astype(BF16)
                        out_ref[g, b * columns : (b + 1) * columns, :] = rounded
                        if keep_error:
                            error_ref[at] = grad[at] - rounded.astype(F32)
                        lines.append(jnp.sum(curv[at], axis=0, keepdims=True))
                    lines.append(jnp.zeros((PAD - owned, width), F32))
                    out_ref[g, owned * columns :, :] = jnp.concatenate(lines, axis=0).astype(BF16)

    grad_shape = (local_blocks, columns, width)
    curv_shape = (local_blocks, 8, width)
    whole = lambda shape: pl.BlockSpec(shape, lambda i, s, d: (0,) * len(shape))
    in_specs = [
        pl.BlockSpec((step, kt, rows, width), lambda i, s, d: (s[0] * steps + i, 0, 0, 0)),
        pl.BlockSpec((per_step, height, rows), lambda i, s, d: (i, 0, 0)),
    ]
    extra = before if last else () if carried is None else (carried,)
    in_specs += [whole(x.shape) for x in extra]
    if last:
        out_shape = [jax.ShapeDtypeStruct((groups, owned * columns + PAD, width), BF16)]
        if keep_error:
            out_shape.append(jax.ShapeDtypeStruct(grad_shape, F32))
        out_specs = [whole(x.shape) for x in out_shape]
        scratch = [pltpu.VMEM(grad_shape, F32), pltpu.VMEM(curv_shape, F32)]
    else:
        out_shape = [jax.ShapeDtypeStruct(grad_shape, F32), jax.ShapeDtypeStruct(curv_shape, F32)]
        out_specs = [whole(grad_shape), whole(curv_shape)]
        scratch = []
    return pl.pallas_call(
        kernel,
        grid_spec=pltpu.PrefetchScalarGridSpec(
            num_scalar_prefetch=2,
            grid=(steps,),
            in_specs=in_specs,
            out_specs=out_specs,
            scratch_shapes=scratch,
        ),
        out_shape=out_shape,
        compiler_params=params(),
    )(scalars, ids, tiles, scaled, *extra)


def update(parts, exact, known, copies):
    sources, height, width = parts.shape
    owned, columns, _ = exact.shape

    def kernel(parts_ref, exact_ref, *refs):
        new_ref, sent_ref = refs[-2:]

        def total(lo, hi):
            value = parts_ref[0, lo:hi, :].astype(F32)
            for s in range(1, sources):
                value = value + parts_ref[s, lo:hi, :].astype(F32)
            return value

        curvature = total(owned * columns, height)
        for b in range(owned):
            gradient = total(b * columns, (b + 1) * columns)
            coef = exact_ref[b]
            new = coef + STEP_SIZE * (gradient - RIDGE * coef) / (curvature[b : b + 1] + RIDGE)
            new_ref[b] = new
            if known is not None:
                new = new - refs[0][b].astype(F32)
            for c in range(copies):
                sent_ref[c, b] = new.astype(BF16)

    return pl.pallas_call(
        kernel,
        out_shape=[
            jax.ShapeDtypeStruct(exact.shape, F32),
            jax.ShapeDtypeStruct((copies,) + exact.shape, BF16),
        ],
        compiler_params=params(),
    )(parts, exact, *(() if known is None else (known,)))


def finish(known, change):
    blocks, columns, width = known.shape
    step = 16

    def kernel(known_ref, change_ref, out_ref):
        for b in range(step):
            value = known_ref[b].astype(F32) + change_ref[b].astype(F32)
            out_ref[:, b * width : (b + 1) * width] = value

    return pl.pallas_call(
        kernel,
        grid=(blocks // step,),
        in_specs=[pl.BlockSpec((step, columns, width), lambda i: (i, 0, 0))] * 2,
        out_specs=pl.BlockSpec((columns, step * width), lambda i: (0, i)),
        out_shape=jax.ShapeDtypeStruct((columns, blocks * width), F32),
        compiler_params=params(),
    )(known, change)


def make_body(n_row, n_feat):
    n_yz = n_feat // 2
    chips = [[2 * i + core for i in range(n_yz)] for core in range(2)]
    other_core = [(i, i ^ 1) for i in range(n_feat)]

    def swap_core(x):
        return lax.ppermute(x, "feat", other_core)

    def exchange_feat(x):
        return lax.all_to_all(x, "feat", 0, 0, axis_index_groups=chips, tiled=True)

    def exchange_row(x):
        return lax.all_to_all(x, "row", 0, 0, tiled=True)

    def body(design_tiles, block_ids, responses, live_groups, start_coef):
        row = lax.axis_index("row")
        feat = lax.axis_index("feat")
        core, yz = feat % 2, feat // 2
        _, owners, slots, kt, rows, width = design_tiles.shape
        row_blocks = owners * slots
        features, columns = start_coef.shape
        local_blocks = features // width
        tiles = design_tiles.reshape(row_blocks, kt, rows, width)
        resp_t = responses.reshape(row_blocks, rows, columns).swapaxes(1, 2)
        start_t = start_coef.T
        ids = lax.dynamic_index_in_dim(block_ids, row, 0, keepdims=False).reshape(-1)
        ids = (ids - feat * local_blocks).astype(jnp.int32)
        share = row_blocks // n_feat
        mine = core * n_yz + yz
        live = lax.dynamic_index_in_dim(live_groups, row, 0, keepdims=False)
        flag = live[mine * share // slots]
        here = jnp.stack([core, flag, mine]).astype(jnp.int32)
        there = jnp.stack([1 - core, flag, mine]).astype(jnp.int32)
        owned = local_blocks // n_row
        own = lax.dynamic_slice_in_dim(start_t, row * owned * width, owned * width, 1)
        own = own.reshape(columns, owned, width).swapaxes(0, 1)

        exact, known, own_known, carried = own, coef_blocks(start_t), None, None
        for iteration in range(ITERS):
            ends = iteration == ITERS - 1
            sent = predict_half(there, ids, tiles, known, F32)
            arrived = swap_core(sent)
            kept = predict_half(here, ids, tiles, known, F32)
            pair = (kept + arrived).astype(BF16)
            parts = exchange_feat(pair).reshape(n_yz, share, columns, rows)
            scaled = exchange_feat(weigh(here, parts, resp_t, n_yz))
            scaled_there = swap_core(scaled)
            before = gradient_half(here, ids, tiles, scaled, local_blocks, n_row, carried)
            partial, *error = gradient_half(
                there, ids, tiles, scaled_there, local_blocks, n_row, None, before, not ends
            )
            carried = None if ends else error[0]
            exact, sent = update(exchange_row(partial), exact, own_known, n_row)
            own_known = sent[0]
            gathered = exchange_row(sent).reshape(local_blocks, columns, width)
            if ends:
                return finish(known, gathered).T
            known = gathered

    return body


def solution(mesh):
    in_specs = (
        P("row", None, None, "feat", None, None),
        P(None, None, None, "feat"),
        P("row", None, None, None, None),
        P(),
        P("feat", None),
    )
    return jax.shard_map(
        make_body(mesh.shape["row"], mesh.shape["feat"]),
        mesh=mesh,
        in_specs=in_specs,
        out_specs=P("feat", None),
        check_vma=False,
    )
```

```python
import jax
import jax.numpy as jnp
from jax import lax
from jax.experimental import pallas as pl
from jax.experimental.pallas import tpu as pltpu
from jax.sharding import PartitionSpec as P

ITERS = 2
STEP_SIZE = 0.25
RIDGE = 0.05
F32 = jnp.float32
BF16 = jnp.bfloat16
VMEM_LIMIT = 16 * 1024 * 1024

LANES = 128
PAD = 16


def params():
    return pltpu.CompilerParams(vmem_limit_bytes=VMEM_LIMIT)


def whole(count, scalars):
    smem = pl.BlockSpec(memory_space=pltpu.SMEM)
    vmem = pl.BlockSpec(memory_space=pltpu.VMEM)
    return [smem] * scalars + [vmem] * count


def coef_blocks(start_t):
    columns, features = start_t.shape
    blocks = features // LANES

    def kernel(start_ref, out_ref):
        for b in range(blocks):
            out_ref[b] = start_ref[:, b * LANES : (b + 1) * LANES].astype(BF16)

    return pl.pallas_call(
        kernel,
        in_specs=whole(1, 0),
        out_specs=whole(1, 0)[0],
        out_shape=jax.ShapeDtypeStruct((blocks, columns, LANES), BF16),
        compiler_params=params(),
    )(start_t)


def side(scalars_ref, other):
    return 1 - scalars_ref[0] if other else scalars_ref[0]


def predict_half(scalars, ids, tiles, coef, other):
    row_blocks, kt, rows, width = tiles.shape
    columns = coef.shape[1]
    half = row_blocks // 2
    step = 8

    def kernel(scalars_ref, ids_ref, tiles_ref, coef_ref, out_ref):
        base = side(scalars_ref, other) * half

        @pl.loop(0, half // step)
        def _(i):
            for r in range(step):
                at = i * step + r
                row_block = base + at
                picked = [coef_ref[ids_ref[row_block * kt + k]] for k in range(kt)]
                placed = [tiles_ref[row_block, k] for k in range(kt)]
                out_ref[at] = lax.dot_general(
                    jnp.concatenate(picked, axis=1),
                    jnp.concatenate(placed, axis=1),
                    (((1,), (1,)), ((), ())),
                    preferred_element_type=F32,
                )

    return pl.pallas_call(
        kernel,
        in_specs=whole(2, 2),
        out_specs=whole(1, 0)[0],
        out_shape=jax.ShapeDtypeStruct((half, columns, rows), F32),
        compiler_params=params(),
    )(scalars, ids, tiles, coef)


def weigh(scalars, parts, resp_t, copies):
    sources, count, columns, rows = parts.shape
    threshold = 1.4 * columns**0.5
    height = count * columns + PAD

    def kernel(scalars_ref, parts_ref, resp_ref, out_ref):
        flag = scalars_ref[1].astype(F32)
        first = scalars_ref[2] * count
        lines = []
        for r in range(count):
            predicted = parts_ref[0, r].astype(F32)
            for s in range(1, sources):
                predicted = predicted + parts_ref[s, r].astype(F32)
            residual = resp_ref[first + r].astype(F32) - predicted
            norm = jnp.sqrt(jnp.sum(residual * residual, axis=0, keepdims=True))
            weight = flag * threshold / jnp.maximum(norm, threshold)
            scaled = (weight * residual).astype(BF16)
            for c in range(copies):
                out_ref[c, r * columns : (r + 1) * columns, :] = scaled
            lines.append(weight)
        lines.append(jnp.zeros((PAD - count, rows), F32))
        tail = jnp.concatenate(lines, axis=0).astype(BF16)
        for c in range(copies):
            out_ref[c, count * columns :, :] = tail

    return pl.pallas_call(
        kernel,
        in_specs=whole(2, 1),
        out_specs=whole(1, 0)[0],
        out_shape=jax.ShapeDtypeStruct((copies, height, rows), BF16),
        compiler_params=params(),
    )(scalars, parts, resp_t)


def gradient_half(scalars, ids, tiles, scaled, other, local_blocks, groups, before, keep_error):
    row_blocks, kt, rows, width = tiles.shape
    sources, height, _ = scaled.shape
    half = row_blocks // 2
    count = half // sources
    columns = (height - PAD) // count
    owned = local_blocks // groups
    n_before = len(before)

    def kernel(scalars_ref, ids_ref, tiles_ref, scaled_ref, *refs):
        before_refs, refs = refs[:n_before], refs[n_before:]
        if other:
            out_ref = refs[0]
            error_ref = refs[1] if keep_error else None
        grad, curv = refs[-2:]
        base = side(scalars_ref, other) * half
        for ref, start in zip((grad, curv), list(before_refs) + [None] * (2 - n_before)):
            ref[...] = jnp.zeros_like(ref) if start is None else start[...]

        @pl.loop(0, sources)
        def _(p):
            tail = scaled_ref[p, count * columns :, :].astype(F32)
            for r in range(count):
                row_block = base + p * count + r
                weights = jnp.broadcast_to(tail[r : r + 1, :], (rows, rows)).T
                placed = [tiles_ref[row_block, k] for k in range(kt)]
                sums = jnp.dot(
                    scaled_ref[p, r * columns : (r + 1) * columns, :],
                    jnp.concatenate(placed, axis=1),
                    preferred_element_type=F32,
                )
                for k in range(kt):
                    block = ids_ref[row_block * kt + k]
                    grad[block] += sums[:, k * width : (k + 1) * width]
                    wide = placed[k].astype(F32)
                    square = wide * wide * weights
                    curv[block] += jnp.sum(square.reshape(rows // 8, 8, width), axis=0)

        if other:

            @pl.loop(0, groups)
            def _(g):
                lines = []
                for b in range(owned):
                    at = g * owned + b
                    rounded = grad[at].astype(BF16)
                    out_ref[g, b * columns : (b + 1) * columns, :] = rounded
                    if keep_error:
                        error_ref[at] = grad[at] - rounded.astype(F32)
                    lines.append(jnp.sum(curv[at], axis=0, keepdims=True))
                lines.append(jnp.zeros((PAD - owned, width), F32))
                out_ref[g, owned * columns :, :] = jnp.concatenate(lines, axis=0).astype(BF16)

    grad_shape = (local_blocks, columns, width)
    curv_shape = (local_blocks, 8, width)
    out_shape, scratch = [], []
    if other:
        out_shape.append(jax.ShapeDtypeStruct((groups, owned * columns + PAD, width), BF16))
        if keep_error:
            out_shape.append(jax.ShapeDtypeStruct(grad_shape, F32))
        scratch = [pltpu.VMEM(grad_shape, F32), pltpu.VMEM(curv_shape, F32)]
    else:
        out_shape = [jax.ShapeDtypeStruct(grad_shape, F32), jax.ShapeDtypeStruct(curv_shape, F32)]
    return pl.pallas_call(
        kernel,
        in_specs=whole(2 + n_before, 2),
        out_specs=whole(len(out_shape), 0),
        out_shape=out_shape,
        scratch_shapes=scratch,
        compiler_params=params(),
    )(scalars, ids, tiles, scaled, *before)


def update(scalars, parts, exact, known, copies, owned):
    sources, height, width = parts.shape
    columns = (height - PAD) // owned
    shape = (owned, columns, width)
    first = known is None

    def kernel(scalars_ref, parts_ref, exact_ref, *refs):
        sent_ref = refs[-1]

        def total(lo, hi):
            value = parts_ref[0, lo:hi, :].astype(F32)
            for s in range(1, sources):
                value = value + parts_ref[s, lo:hi, :].astype(F32)
            return value

        curvature = total(owned * columns, height)
        for b in range(owned):
            gradient = total(b * columns, (b + 1) * columns)
            if first:
                at = pl.multiple_of((scalars_ref[3] * owned + b) * width, width)
                coef = exact_ref[:, pl.ds(at, width)]
            else:
                coef = exact_ref[b]
            new = coef + STEP_SIZE * (gradient - RIDGE * coef) / (curvature[b : b + 1] + RIDGE)
            if first:
                refs[0][b] = new
            else:
                new = new - refs[0][0, b].astype(F32)
            for c in range(copies):
                sent_ref[c, b] = new.astype(BF16)

    out_shape = [jax.ShapeDtypeStruct((copies,) + shape, BF16)]
    if first:
        out_shape.insert(0, jax.ShapeDtypeStruct(shape, F32))
    return pl.pallas_call(
        kernel,
        in_specs=whole(2 + (not first), 1),
        out_specs=whole(len(out_shape), 0),
        out_shape=out_shape,
        compiler_params=params(),
    )(scalars, parts, exact, *(() if first else (known,)))


def finish(known, change):
    blocks, columns, width = known.shape
    step = 16

    def kernel(known_ref, change_ref, out_ref):
        for b in range(step):
            value = known_ref[b].astype(F32) + change_ref[b].astype(F32)
            out_ref[:, b * width : (b + 1) * width] = value

    return pl.pallas_call(
        kernel,
        grid=(blocks // step,),
        in_specs=[pl.BlockSpec((step, columns, width), lambda i: (i, 0, 0))] * 2,
        out_specs=pl.BlockSpec((columns, step * width), lambda i: (0, i)),
        out_shape=jax.ShapeDtypeStruct((columns, blocks * width), F32),
        compiler_params=params(),
    )(known, change)


def make_body(n_row, n_feat):
    n_yz = n_feat // 2
    chips = [[2 * i + core for i in range(n_yz)] for core in range(2)]
    other_core = [(i, i ^ 1) for i in range(n_feat)]

    def swap_core(x):
        return lax.ppermute(x, "feat", other_core)

    def exchange_feat(x):
        return lax.all_to_all(x, "feat", 0, 0, axis_index_groups=chips, tiled=True)

    def exchange_row(x):
        return lax.all_to_all(x, "row", 0, 0, tiled=True)

    def body(design_tiles, block_ids, responses, live_groups, start_coef):
        row = lax.axis_index("row")
        feat = lax.axis_index("feat")
        core, yz = feat % 2, feat // 2
        _, owners, slots, kt, rows, width = design_tiles.shape
        row_blocks = owners * slots
        features, columns = start_coef.shape
        local_blocks = features // width
        tiles = design_tiles.reshape(row_blocks, kt, rows, width)
        resp_t = responses.reshape(row_blocks, rows, columns).swapaxes(1, 2)
        start_t = start_coef.T
        ids = lax.dynamic_index_in_dim(block_ids, row, 0, keepdims=False).reshape(-1)
        ids = (ids - feat * local_blocks).astype(jnp.int32)
        share = row_blocks // n_feat
        mine = core * n_yz + yz
        live = lax.dynamic_index_in_dim(live_groups, row, 0, keepdims=False)
        flag = live[mine * share // slots]
        scalars = jnp.stack([core, flag, mine, row]).astype(jnp.int32)
        owned = local_blocks // n_row

        known, exact, sent, carried = coef_blocks(start_t), start_t, None, ()
        for iteration in range(ITERS):
            ends = iteration == ITERS - 1
            arrived = swap_core(predict_half(scalars, ids, tiles, known, True))
            kept = predict_half(scalars, ids, tiles, known, False)
            pair = (kept + arrived).astype(BF16)
            parts = exchange_feat(pair).reshape(n_yz, share, columns, rows)
            scaled = exchange_feat(weigh(scalars, parts, resp_t, n_yz))
            scaled_there = swap_core(scaled)
            before = gradient_half(
                scalars, ids, tiles, scaled, False, local_blocks, n_row, carried, False
            )
            partial, *carried = gradient_half(
                scalars, ids, tiles, scaled_there, True, local_blocks, n_row, before, not ends
            )
            *new, sent = update(scalars, exchange_row(partial), exact, sent, n_row, owned)
            gathered = exchange_row(sent).reshape(local_blocks, columns, width)
            if ends:
                return finish(known, gathered).T
            known, exact = gathered, new[0]

    return body


def solution(mesh):
    in_specs = (
        P("row", None, None, "feat", None, None),
        P(None, None, None, "feat"),
        P("row", None, None, None, None),
        P(),
        P("feat", None),
    )
    return jax.shard_map(
        make_body(mesh.shape["row"], mesh.shape["feat"]),
        mesh=mesh,
        in_specs=in_specs,
        out_specs=P("feat", None),
        check_vma=False,
    )
```

```python
import jax
import jax.numpy as jnp
from jax import lax
from jax.experimental import pallas as pl
from jax.experimental.pallas import tpu as pltpu
from jax.sharding import PartitionSpec as P

ITERS = 2
STEP_SIZE = 0.25
RIDGE = 0.05
F32 = jnp.float32
BF16 = jnp.bfloat16
VMEM_LIMIT = 16 * 1024 * 1024
FIRST_LIMIT = 50 * 1024 * 1024

LANES = 128
PAD = 16


def params(limit=VMEM_LIMIT):
    return pltpu.CompilerParams(vmem_limit_bytes=limit)


def whole(count, scalars):
    smem = pl.BlockSpec(memory_space=pltpu.SMEM)
    vmem = pl.BlockSpec(memory_space=pltpu.VMEM)
    return [smem] * scalars + [vmem] * count


def place():
    feat = lax.axis_index("feat")
    return lax.axis_index("row"), feat % 2, feat // 2


def side(other):
    core = lax.axis_index("feat") % 2
    return 1 - core if other else core


def predict_block(ids_ref, tiles_ref, coef_ref, at, row_block, kt):
    picked = [coef_ref[ids_ref[row_block * kt + k]] for k in range(kt)]
    placed = [tiles_ref[at, k] for k in range(kt)]
    return lax.dot_general(
        jnp.concatenate(picked, axis=1),
        jnp.concatenate(placed, axis=1),
        (((1,), (1,)), ((), ())),
        preferred_element_type=F32,
    )


def predict_stream(ids, tiles, other, start_t, coef=None):
    row_blocks, kt, rows, width = tiles.shape
    columns, features = start_t.shape
    blocks = features // width
    half = row_blocks // 2
    step = 8
    pieces = half // step
    coef_pieces = 4
    share = features // coef_pieces
    makes = coef is None

    def kernel(ids_ref, tiles_hbm, source_ref, out_ref, *refs):
        if makes:
            coef_ref, held, tile_sem, start_ref, start_sem = refs
        else:
            coef_ref, (held, tile_sem) = source_ref, refs
        base = side(other) * half
        starts, copies = [], []
        if makes:
            for p in range(coef_pieces):
                at = pl.ds(p * share, share)
                starts.append(
                    pltpu.make_async_copy(source_ref.at[:, at], start_ref.at[:, at], start_sem.at[p])
                )
        for p in range(pieces):
            copies.append(
                pltpu.make_async_copy(
                    tiles_hbm.at[pl.ds(base + p * step, step)],
                    held.at[pl.ds(p * step, step)],
                    tile_sem.at[p],
                )
            )
        for copy in starts + copies:
            copy.start()
        for p in range(len(starts)):
            starts[p].wait()
            for b in range(p * blocks // coef_pieces, (p + 1) * blocks // coef_pieces):
                coef_ref[b] = start_ref[:, b * width : (b + 1) * width].astype(BF16)
        for p in range(pieces):
            copies[p].wait()
            for r in range(step):
                at = p * step + r
                out_ref[at] = predict_block(ids_ref, held, coef_ref, at, base + at, kt)

    hbm = pl.BlockSpec(memory_space=pltpu.HBM)
    out_shape = [jax.ShapeDtypeStruct((half, columns, rows), F32)]
    scratch = [pltpu.VMEM((half, kt, rows, width), BF16), pltpu.SemaphoreType.DMA((pieces,))]
    if makes:
        out_shape.append(jax.ShapeDtypeStruct((blocks, columns, width), BF16))
        scratch += [pltpu.VMEM(start_t.shape, F32), pltpu.SemaphoreType.DMA((coef_pieces,))]
    return pl.pallas_call(
        kernel,
        in_specs=whole(0, 1) + [hbm] + ([hbm] if makes else whole(1, 0)),
        out_specs=whole(len(out_shape), 0),
        out_shape=out_shape,
        scratch_shapes=scratch,
        compiler_params=params(FIRST_LIMIT),
    )(ids, tiles, start_t if makes else coef)


def predict_half(ids, tiles, coef, other):
    row_blocks, kt, rows, width = tiles.shape
    columns = coef.shape[1]
    half = row_blocks // 2
    step = 8

    def kernel(ids_ref, tiles_ref, coef_ref, out_ref):
        base = side(other) * half

        @pl.loop(0, half // step)
        def _(i):
            for r in range(step):
                at = i * step + r
                out_ref[at] = predict_block(ids_ref, tiles_ref, coef_ref, base + at, base + at, kt)

    return pl.pallas_call(
        kernel,
        in_specs=whole(2, 1),
        out_specs=whole(1, 0)[0],
        out_shape=jax.ShapeDtypeStruct((half, columns, rows), F32),
        compiler_params=params(),
    )(ids, tiles, coef)


def weigh(n_feat, live, parts, resp_t, copies):
    sources, count, columns, rows = parts.shape
    threshold = 1.4 * columns**0.5
    height = count * columns + PAD

    slots = resp_t.shape[0] // live.shape[1]

    def kernel(live_ref, parts_ref, resp_ref, out_ref):
        row, core, chip = place()
        first = (core * (n_feat // 2) + chip) * count
        flag = live_ref[row, first // slots].astype(F32)
        lines = []
        for r in range(count):
            predicted = parts_ref[0, r].astype(F32)
            for s in range(1, sources):
                predicted = predicted + parts_ref[s, r].astype(F32)
            residual = resp_ref[first + r].astype(F32) - predicted
            norm = jnp.sqrt(jnp.sum(residual * residual, axis=0, keepdims=True))
            weight = flag * threshold / jnp.maximum(norm, threshold)
            scaled = (weight * residual).astype(BF16)
            for c in range(copies):
                out_ref[c, r * columns : (r + 1) * columns, :] = scaled
            lines.append(weight)
        lines.append(jnp.zeros((PAD - count, rows), F32))
        tail = jnp.concatenate(lines, axis=0).astype(BF16)
        for c in range(copies):
            out_ref[c, count * columns :, :] = tail

    return pl.pallas_call(
        kernel,
        in_specs=whole(2, 1),
        out_specs=whole(1, 0)[0],
        out_shape=jax.ShapeDtypeStruct((copies, height, rows), BF16),
        compiler_params=params(),
    )(live, parts, resp_t)


def gradient_half(ids, tiles, scaled, other, local_blocks, groups, before, keep_error):
    row_blocks, kt, rows, width = tiles.shape
    sources, height, _ = scaled.shape
    half = row_blocks // 2
    count = half // sources
    columns = (height - PAD) // count
    owned = local_blocks // groups
    n_before = len(before)

    def kernel(ids_ref, tiles_ref, scaled_ref, *refs):
        before_refs, refs = refs[:n_before], refs[n_before:]
        if other:
            out_ref = refs[0]
            error_ref = refs[1] if keep_error else None
        grad, curv = refs[-2:]
        base = side(other) * half
        for ref, start in zip((grad, curv), list(before_refs) + [None] * (2 - n_before)):
            ref[...] = jnp.zeros_like(ref) if start is None else start[...]

        @pl.loop(0, sources)
        def _(p):
            tail = scaled_ref[p, count * columns :, :].astype(F32)
            for r in range(count):
                row_block = base + p * count + r
                weights = jnp.broadcast_to(tail[r : r + 1, :], (rows, rows)).T
                placed = [tiles_ref[row_block, k] for k in range(kt)]
                sums = jnp.dot(
                    scaled_ref[p, r * columns : (r + 1) * columns, :],
                    jnp.concatenate(placed, axis=1),
                    preferred_element_type=F32,
                )
                for k in range(kt):
                    block = ids_ref[row_block * kt + k]
                    grad[block] += sums[:, k * width : (k + 1) * width]
                    wide = placed[k].astype(F32)
                    square = wide * wide * weights
                    curv[block] += jnp.sum(square.reshape(rows // 8, 8, width), axis=0)

        if other:

            @pl.loop(0, groups)
            def _(g):
                lines = []
                for b in range(owned):
                    at = g * owned + b
                    rounded = grad[at].astype(BF16)
                    out_ref[g, b * columns : (b + 1) * columns, :] = rounded
                    if keep_error:
                        error_ref[at] = grad[at] - rounded.astype(F32)
                    lines.append(jnp.sum(curv[at], axis=0, keepdims=True))
                lines.append(jnp.zeros((PAD - owned, width), F32))
                out_ref[g, owned * columns :, :] = jnp.concatenate(lines, axis=0).astype(BF16)

    grad_shape = (local_blocks, columns, width)
    curv_shape = (local_blocks, 8, width)
    out_shape, scratch = [], []
    if other:
        out_shape.append(jax.ShapeDtypeStruct((groups, owned * columns + PAD, width), BF16))
        if keep_error:
            out_shape.append(jax.ShapeDtypeStruct(grad_shape, F32))
        scratch = [pltpu.VMEM(grad_shape, F32), pltpu.VMEM(curv_shape, F32)]
    else:
        out_shape = [jax.ShapeDtypeStruct(grad_shape, F32), jax.ShapeDtypeStruct(curv_shape, F32)]
    return pl.pallas_call(
        kernel,
        in_specs=whole(2 + n_before, 1),
        out_specs=whole(len(out_shape), 0),
        out_shape=out_shape,
        scratch_shapes=scratch,
        compiler_params=params(),
    )(ids, tiles, scaled, *before)


def update(parts, exact, known, copies, owned):
    sources, height, width = parts.shape
    columns = (height - PAD) // owned
    shape = (owned, columns, width)
    first = known is None

    def kernel(parts_ref, exact_ref, *refs):
        sent_ref = refs[-1]

        def total(lo, hi):
            value = parts_ref[0, lo:hi, :].astype(F32)
            for s in range(1, sources):
                value = value + parts_ref[s, lo:hi, :].astype(F32)
            return value

        curvature = total(owned * columns, height)
        for b in range(owned):
            gradient = total(b * columns, (b + 1) * columns)
            if first:
                at = pl.multiple_of((lax.axis_index("row") * owned + b) * width, width)
                coef = exact_ref[:, pl.ds(at, width)]
            else:
                coef = exact_ref[b]
            new = coef + STEP_SIZE * (gradient - RIDGE * coef) / (curvature[b : b + 1] + RIDGE)
            if first:
                refs[0][b] = new
            else:
                new = new - refs[0][0, b].astype(F32)
            for c in range(copies):
                sent_ref[c, b] = new.astype(BF16)

    out_shape = [jax.ShapeDtypeStruct((copies,) + shape, BF16)]
    if first:
        out_shape.insert(0, jax.ShapeDtypeStruct(shape, F32))
    return pl.pallas_call(
        kernel,
        in_specs=whole(2 + (not first), 0),
        out_specs=whole(len(out_shape), 0),
        out_shape=out_shape,
        compiler_params=params(),
    )(parts, exact, *(() if first else (known,)))


def finish(known, change):
    blocks, columns, width = known.shape
    pieces = 4
    step = blocks // pieces

    def kernel(known_ref, change_ref, out_hbm, held, sem):
        copies = []
        for p in range(pieces):
            for b in range(p * step, (p + 1) * step):
                held[:, b * width : (b + 1) * width] = known_ref[b].astype(F32) + change_ref[b].astype(F32)
            at = pl.ds(p * step * width, step * width)
            copies.append(pltpu.make_async_copy(held.at[:, at], out_hbm.at[:, at], sem.at[p]))
            copies[p].start()
        for copy in copies:
            copy.wait()

    shape = (columns, blocks * width)
    return pl.pallas_call(
        kernel,
        in_specs=whole(2, 0),
        out_specs=pl.BlockSpec(memory_space=pltpu.HBM),
        out_shape=jax.ShapeDtypeStruct(shape, F32),
        scratch_shapes=[pltpu.VMEM(shape, F32), pltpu.SemaphoreType.DMA((pieces,))],
        compiler_params=params(),
    )(known, change)


def make_body(n_row, n_feat):
    n_yz = n_feat // 2
    chips = [[2 * i + core for i in range(n_yz)] for core in range(2)]
    other_core = [(i, i ^ 1) for i in range(n_feat)]

    def swap_core(x):
        return lax.ppermute(x, "feat", other_core)

    def exchange_feat(x):
        return lax.all_to_all(x, "feat", 0, 0, axis_index_groups=chips, tiled=True)

    def exchange_row(x):
        return lax.all_to_all(x, "row", 0, 0, tiled=True)

    def body(design_tiles, block_ids, responses, live_groups, start_coef):
        row = lax.axis_index("row")
        feat = lax.axis_index("feat")
        _, owners, slots, kt, rows, width = design_tiles.shape
        row_blocks = owners * slots
        features, columns = start_coef.shape
        local_blocks = features // width
        tiles = design_tiles.reshape(row_blocks, kt, rows, width)
        resp_t = responses.reshape(row_blocks, rows, columns).swapaxes(1, 2)
        start_t = start_coef.T
        ids = lax.dynamic_index_in_dim(block_ids, row, 0, keepdims=False).reshape(-1)
        ids = (ids - feat * local_blocks).astype(jnp.int32)
        share = row_blocks // n_feat
        owned = local_blocks // n_row

        known = None
        exact, sent, carried = start_t, None, ()
        for iteration in range(ITERS):
            ends = iteration == ITERS - 1
            if iteration == 0:
                ahead, known = predict_stream(ids, tiles, True, start_t)
                arrived = swap_core(ahead)
                [kept] = predict_stream(ids, tiles, False, start_t, known)
            else:
                arrived = swap_core(predict_half(ids, tiles, known, True))
                kept = predict_half(ids, tiles, known, False)
            pair = (kept + arrived).astype(BF16)
            parts = exchange_feat(pair).reshape(n_yz, share, columns, rows)
            scaled = exchange_feat(weigh(n_feat, live_groups, parts, resp_t, n_yz))
            scaled_there = swap_core(scaled)
            before = gradient_half(
                ids, tiles, scaled, False, local_blocks, n_row, carried, False
            )
            partial, *carried = gradient_half(
                ids, tiles, scaled_there, True, local_blocks, n_row, before, not ends
            )
            *new, sent = update(exchange_row(partial), exact, sent, n_row, owned)
            gathered = exchange_row(sent).reshape(local_blocks, columns, width)
            if ends:
                return finish(known, gathered).T
            known, exact = gathered, new[0]

    return body


def solution(mesh):
    in_specs = (
        P("row", None, None, "feat", None, None),
        P(None, None, None, "feat"),
        P("row", None, None, None, None),
        P(),
        P("feat", None),
    )
    return jax.shard_map(
        make_body(mesh.shape["row"], mesh.shape["feat"]),
        mesh=mesh,
        in_specs=in_specs,
        out_specs=P("feat", None),
        check_vma=False,
    )
```

```python
import jax
import jax.numpy as jnp
from jax import lax
from jax.experimental import pallas as pl
from jax.experimental.pallas import tpu as pltpu
from jax.sharding import PartitionSpec as P

ITERS = 2
STEP_SIZE = 0.25
RIDGE = 0.05
F32 = jnp.float32
BF16 = jnp.bfloat16
VMEM_LIMIT = 16 * 1024 * 1024
FIRST_LIMIT = 50 * 1024 * 1024

LANES = 128
PAD = 16


def params(limit=VMEM_LIMIT):
    return pltpu.CompilerParams(vmem_limit_bytes=limit)


def whole(count, scalars):
    smem = pl.BlockSpec(memory_space=pltpu.SMEM)
    vmem = pl.BlockSpec(memory_space=pltpu.VMEM)
    return [smem] * scalars + [vmem] * count


def place():
    feat = lax.axis_index("feat")
    return lax.axis_index("row"), feat % 2, feat // 2


def side(other):
    core = lax.axis_index("feat") % 2
    return 1 - core if other else core


def predict_pair(ids_ref, tiles_ref, coef_ref, out_ref, put, at, row_block, kt):
    picked, placed = [], []
    for r in range(2):
        first = (row_block + r) * kt
        picked.append(jnp.concatenate([coef_ref[ids_ref[first + k]] for k in range(kt)], axis=1))
        placed.append(jnp.concatenate([tiles_ref[at + r, k] for k in range(kt)], axis=1))
    both = lax.dot_general(
        jnp.concatenate(picked, axis=0),
        jnp.concatenate(placed, axis=0),
        (((1,), (1,)), ((), ())),
        preferred_element_type=F32,
    )
    columns, rows = picked[0].shape[0], placed[0].shape[0]
    out_ref[put] = both[:columns, :rows]
    out_ref[put + 1] = both[columns:, rows:]


def predict_first(ids, tiles, start_t):
    row_blocks, kt, rows, width = tiles.shape
    columns, features = start_t.shape
    blocks = features // width
    half = row_blocks // 2
    step = 8
    pieces = half // step
    coef_pieces = 4
    share = features // coef_pieces

    def kernel(ids_ref, tiles_hbm, start_hbm, out_ref, coef_ref, held, tile_sem, start_ref, start_sem):
        base = side(True) * half
        starts, copies = [], []
        for p in range(coef_pieces):
            at = pl.ds(p * share, share)
            starts.append(
                pltpu.make_async_copy(start_hbm.at[:, at], start_ref.at[:, at], start_sem.at[p])
            )
        for p in range(pieces):
            copies.append(
                pltpu.make_async_copy(
                    tiles_hbm.at[pl.ds(base + p * step, step)],
                    held.at[pl.ds(p * step, step)],
                    tile_sem.at[p],
                )
            )
        for copy in starts + copies:
            copy.start()
        for p in range(coef_pieces):
            starts[p].wait()
            for b in range(p * blocks // coef_pieces, (p + 1) * blocks // coef_pieces):
                coef_ref[b] = start_ref[:, b * width : (b + 1) * width].astype(BF16)
        for p in range(pieces):
            copies[p].wait()
            for r in range(0, step, 2):
                at = p * step + r
                predict_pair(ids_ref, held, coef_ref, out_ref, at, at, base + at, kt)

    hbm = pl.BlockSpec(memory_space=pltpu.HBM)
    return pl.pallas_call(
        kernel,
        in_specs=whole(0, 1) + [hbm, hbm],
        out_specs=whole(2, 0),
        out_shape=[
            jax.ShapeDtypeStruct((half, columns, rows), F32),
            jax.ShapeDtypeStruct((blocks, columns, width), BF16),
        ],
        scratch_shapes=[
            pltpu.VMEM((half, kt, rows, width), BF16),
            pltpu.SemaphoreType.DMA((pieces,)),
            pltpu.VMEM(start_t.shape, F32),
            pltpu.SemaphoreType.DMA((coef_pieces,)),
        ],
        compiler_params=params(FIRST_LIMIT),
    )(ids, tiles, start_t)


def predict_half(ids, tiles, coef, other):
    row_blocks, kt, rows, width = tiles.shape
    columns = coef.shape[1]
    half = row_blocks // 2
    step = 16

    def kernel(ids_ref, tiles_ref, coef_ref, out_ref):
        base = side(other) * half

        @pl.loop(0, half // step)
        def _(i):
            for r in range(0, step, 2):
                at = i * step + r
                predict_pair(ids_ref, tiles_ref, coef_ref, out_ref, at, base + at, base + at, kt)

    return pl.pallas_call(
        kernel,
        in_specs=whole(2, 1),
        out_specs=whole(1, 0)[0],
        out_shape=jax.ShapeDtypeStruct((half, columns, rows), F32),
        compiler_params=params(),
    )(ids, tiles, coef)


def weigh(n_feat, live, parts, resp_t, copies):
    sources, count, columns, rows = parts.shape
    threshold = 1.4 * columns**0.5
    height = count * columns + PAD

    slots = resp_t.shape[0] // live.shape[1]

    def kernel(live_ref, parts_ref, resp_ref, out_ref):
        row, core, chip = place()
        first = (core * (n_feat // 2) + chip) * count
        flag = live_ref[row, first // slots].astype(F32)
        lines = []
        for r in range(count):
            predicted = parts_ref[0, r].astype(F32)
            for s in range(1, sources):
                predicted = predicted + parts_ref[s, r].astype(F32)
            residual = resp_ref[first + r].astype(F32) - predicted
            norm = jnp.sqrt(jnp.sum(residual * residual, axis=0, keepdims=True))
            weight = flag * threshold / jnp.maximum(norm, threshold)
            scaled = (weight * residual).astype(BF16)
            for c in range(copies):
                out_ref[c, r * columns : (r + 1) * columns, :] = scaled
            lines.append(weight)
        lines.append(jnp.zeros((PAD - count, rows), F32))
        tail = jnp.concatenate(lines, axis=0).astype(BF16)
        for c in range(copies):
            out_ref[c, count * columns :, :] = tail

    return pl.pallas_call(
        kernel,
        in_specs=whole(2, 1),
        out_specs=whole(1, 0)[0],
        out_shape=jax.ShapeDtypeStruct((copies, height, rows), BF16),
        compiler_params=params(),
    )(live, parts, resp_t)


def gradient_half(ids, tiles, scaled, other, local_blocks, groups, before, keep_error):
    row_blocks, kt, rows, width = tiles.shape
    sources, height, _ = scaled.shape
    half = row_blocks // 2
    count = half // sources
    columns = (height - PAD) // count
    owned = local_blocks // groups
    n_before = len(before)
    turn = 2

    def kernel(ids_ref, tiles_ref, scaled_ref, *refs):
        grad, curv, *out = refs[n_before:]
        base = side(other) * half
        for ref in (grad, curv)[n_before:]:
            ref[...] = jnp.zeros_like(ref)

        def add(p):
            tail = scaled_ref[p, count * columns :, :].astype(F32)
            for r in range(count):
                row_block = base + p * count + r
                weights = jnp.broadcast_to(tail[r : r + 1, :], (rows, rows)).T
                placed = [tiles_ref[row_block, k] for k in range(kt)]
                sums = jnp.dot(
                    scaled_ref[p, r * columns : (r + 1) * columns, :],
                    jnp.concatenate(placed, axis=1),
                    preferred_element_type=F32,
                )
                for k in range(kt):
                    block = ids_ref[row_block * kt + k]
                    grad[block] += sums[:, k * width : (k + 1) * width]
                    wide = placed[k].astype(F32)
                    square = wide * wide * weights
                    curv[block] += jnp.sum(square.reshape(rows // 8, 8, width), axis=0)

        @pl.loop(0, sources // turn)
        def _(i):
            for t in range(turn):
                add(i * turn + t)

        if other:

            @pl.loop(0, groups)
            def _(g):
                lines = []
                for b in range(owned):
                    at = g * owned + b
                    rounded = grad[at].astype(BF16)
                    out[0][g, b * columns : (b + 1) * columns, :] = rounded
                    if keep_error:
                        grad[at] -= rounded.astype(F32)
                    lines.append(jnp.sum(curv[at], axis=0, keepdims=True))
                lines.append(jnp.zeros((PAD - owned, width), F32))
                out[0][g, owned * columns :, :] = jnp.concatenate(lines, axis=0).astype(BF16)

    out_shape = [
        jax.ShapeDtypeStruct((local_blocks, columns, width), F32),
        jax.ShapeDtypeStruct((local_blocks, 8, width), F32),
    ]
    if other:
        out_shape.append(jax.ShapeDtypeStruct((groups, owned * columns + PAD, width), BF16))
    return pl.pallas_call(
        kernel,
        in_specs=whole(2 + n_before, 1),
        out_specs=whole(len(out_shape), 0),
        out_shape=out_shape,
        input_output_aliases={3 + i: i for i in range(n_before)},
        compiler_params=params(),
    )(ids, tiles, scaled, *before)


def update(parts, exact, known, copies, owned):
    sources, height, width = parts.shape
    columns = (height - PAD) // owned
    shape = (owned, columns, width)
    first = known is None

    def kernel(parts_ref, exact_ref, *refs):
        sent_ref = refs[-1]

        def total(lo, hi):
            value = parts_ref[0, lo:hi, :].astype(F32)
            for s in range(1, sources):
                value = value + parts_ref[s, lo:hi, :].astype(F32)
            return value

        curvature = total(owned * columns, height)
        for b in range(owned):
            gradient = total(b * columns, (b + 1) * columns)
            if first:
                at = pl.multiple_of((lax.axis_index("row") * owned + b) * width, width)
                coef = exact_ref[:, pl.ds(at, width)]
            else:
                coef = exact_ref[b]
            new = coef + STEP_SIZE * (gradient - RIDGE * coef) / (curvature[b : b + 1] + RIDGE)
            if first:
                refs[0][b] = new
            else:
                new = new - refs[0][0, b].astype(F32)
            for c in range(copies):
                sent_ref[c, b] = new.astype(BF16)

    out_shape = [jax.ShapeDtypeStruct((copies,) + shape, BF16)]
    if first:
        out_shape.insert(0, jax.ShapeDtypeStruct(shape, F32))
    return pl.pallas_call(
        kernel,
        in_specs=whole(2 + (not first), 0),
        out_specs=whole(len(out_shape), 0),
        out_shape=out_shape,
        compiler_params=params(),
    )(parts, exact, *(() if first else (known,)))


def finish(known, change):
    blocks, columns, width = known.shape
    pieces = 4
    step = blocks // pieces

    def kernel(known_ref, change_ref, out_hbm, held, sem):
        copies = []
        for p in range(pieces):
            for b in range(p * step, (p + 1) * step):
                held[:, b * width : (b + 1) * width] = known_ref[b].astype(F32) + change_ref[b].astype(F32)
            at = pl.ds(p * step * width, step * width)
            copies.append(pltpu.make_async_copy(held.at[:, at], out_hbm.at[:, at], sem.at[p]))
            copies[p].start()
        for copy in copies:
            copy.wait()

    shape = (columns, blocks * width)
    return pl.pallas_call(
        kernel,
        in_specs=whole(2, 0),
        out_specs=pl.BlockSpec(memory_space=pltpu.HBM),
        out_shape=jax.ShapeDtypeStruct(shape, F32),
        scratch_shapes=[pltpu.VMEM(shape, F32), pltpu.SemaphoreType.DMA((pieces,))],
        compiler_params=params(),
    )(known, change)


def make_body(n_row, n_feat):
    n_yz = n_feat // 2
    chips = [[2 * i + core for i in range(n_yz)] for core in range(2)]
    other_core = [(i, i ^ 1) for i in range(n_feat)]

    def swap_core(x):
        return lax.ppermute(x, "feat", other_core)

    def exchange_feat(x):
        return lax.all_to_all(x, "feat", 0, 0, axis_index_groups=chips, tiled=True)

    def exchange_row(x):
        return lax.all_to_all(x, "row", 0, 0, tiled=True)

    def body(design_tiles, block_ids, responses, live_groups, start_coef):
        row = lax.axis_index("row")
        feat = lax.axis_index("feat")
        _, owners, slots, kt, rows, width = design_tiles.shape
        row_blocks = owners * slots
        features, columns = start_coef.shape
        local_blocks = features // width
        tiles = design_tiles.reshape(row_blocks, kt, rows, width)
        resp_t = responses.reshape(row_blocks, rows, columns).swapaxes(1, 2)
        start_t = start_coef.T
        ids = lax.dynamic_index_in_dim(block_ids, row, 0, keepdims=False).reshape(-1)
        ids = (ids - feat * local_blocks).astype(jnp.int32)
        share = row_blocks // n_feat
        owned = local_blocks // n_row

        known = None
        exact, sent, carried = start_t, None, ()
        for iteration in range(ITERS):
            ends = iteration == ITERS - 1
            if iteration == 0:
                ahead, known = predict_first(ids, tiles, start_t)
            else:
                ahead = predict_half(ids, tiles, known, True)
            arrived = swap_core(ahead)
            kept = predict_half(ids, tiles, known, False)
            pair = (kept + arrived).astype(BF16)
            parts = exchange_feat(pair).reshape(n_yz, share, columns, rows)
            scaled = exchange_feat(weigh(n_feat, live_groups, parts, resp_t, n_yz))
            scaled_there = swap_core(scaled)
            before = gradient_half(
                ids, tiles, scaled, False, local_blocks, n_row, carried, False
            )
            error, _, partial = gradient_half(
                ids, tiles, scaled_there, True, local_blocks, n_row, before, not ends
            )
            carried = (error,)
            *new, sent = update(exchange_row(partial), exact, sent, n_row, owned)
            gathered = exchange_row(sent).reshape(local_blocks, columns, width)
            if ends:
                return finish(known, gathered).T
            known, exact = gathered, new[0]

    return body


def solution(mesh):
    in_specs = (
        P("row", None, None, "feat", None, None),
        P(None, None, None, "feat"),
        P("row", None, None, None, None),
        P(),
        P("feat", None),
    )
    return jax.shard_map(
        make_body(mesh.shape["row"], mesh.shape["feat"]),
        mesh=mesh,
        in_specs=in_specs,
        out_specs=P("feat", None),
        check_vma=False,
    )
```

```python
import jax
import jax.numpy as jnp
from jax import lax
from jax.experimental import pallas as pl
from jax.experimental.pallas import tpu as pltpu
from jax.sharding import PartitionSpec as P

ITERS = 2
STEP_SIZE = 0.25
RIDGE = 0.05
F32 = jnp.float32
BF16 = jnp.bfloat16
VMEM_LIMIT = 16 * 1024 * 1024
FIRST_LIMIT = 50 * 1024 * 1024

LANES = 128
PAD = 16


def params(limit=VMEM_LIMIT):
    return pltpu.CompilerParams(vmem_limit_bytes=limit)


def whole(count, scalars):
    smem = pl.BlockSpec(memory_space=pltpu.SMEM)
    vmem = pl.BlockSpec(memory_space=pltpu.VMEM)
    return [smem] * scalars + [vmem] * count


def place(n_feat):
    feat = lax.axis_index("feat")
    return lax.axis_index("row"), lax.rem(feat, 2), lax.div(feat, 2)


def side(other):
    core = lax.axis_index("feat") % 2
    return 1 - core if other else core


def predict_pair(ids_ref, tiles_ref, coef_ref, out_ref, put, at, row_block, kt):
    picked, placed = [], []
    for r in range(2):
        first = (row_block + r) * kt
        picked.append(jnp.concatenate([coef_ref[ids_ref[first + k]] for k in range(kt)], axis=1))
        placed.append(jnp.concatenate([tiles_ref[at + r, k] for k in range(kt)], axis=1))
    both = lax.dot_general(
        jnp.concatenate(picked, axis=0),
        jnp.concatenate(placed, axis=0),
        (((1,), (1,)), ((), ())),
        preferred_element_type=F32,
    )
    columns, rows = picked[0].shape[0], placed[0].shape[0]
    out_ref[put] = both[:columns, :rows]
    out_ref[put + 1] = both[columns:, rows:]


def predict_first(ids, tiles, start_t, owned):
    row_blocks, kt, rows, width = tiles.shape
    columns, features = start_t.shape
    blocks = features // width
    half = row_blocks // 2
    step = 8
    pieces = half // step
    coef_pieces = 4
    share = features // coef_pieces

    def kernel(ids_vmem, tiles_hbm, start_hbm, out_ref, coef_ref, own_ref, *scratch):
        held, tile_sem, start_ref, start_sem, ids_ref, ids_sem = scratch
        base = side(True) * half
        starts, copies = [], []
        ids_copy = pltpu.make_async_copy(ids_vmem, ids_ref, ids_sem)
        for p in range(coef_pieces):
            at = pl.ds(p * share, share)
            starts.append(
                pltpu.make_async_copy(start_hbm.at[:, at], start_ref.at[:, at], start_sem.at[p])
            )
        for p in range(pieces):
            copies.append(
                pltpu.make_async_copy(
                    tiles_hbm.at[pl.ds(base + p * step, step)],
                    held.at[pl.ds(p * step, step)],
                    tile_sem.at[p],
                )
            )
        for copy in starts + [ids_copy] + copies:
            copy.start()
        for p in range(coef_pieces):
            starts[p].wait()
            for b in range(p * blocks // coef_pieces, (p + 1) * blocks // coef_pieces):
                coef_ref[b] = start_ref[:, b * width : (b + 1) * width].astype(BF16)
        for b in range(owned):
            at = pl.multiple_of((lax.axis_index("row") * owned + b) * width, width)
            own_ref[b] = start_ref[:, pl.ds(at, width)]
        ids_copy.wait()
        for p in range(pieces):
            copies[p].wait()
            for r in range(0, step, 2):
                at = p * step + r
                predict_pair(ids_ref, held, coef_ref, out_ref, at, at, base + at, kt)

    hbm = pl.BlockSpec(memory_space=pltpu.HBM)
    return pl.pallas_call(
        kernel,
        in_specs=whole(1, 0) + [hbm, hbm],
        out_specs=whole(3, 0),
        out_shape=[
            jax.ShapeDtypeStruct((half, columns, rows), F32),
            jax.ShapeDtypeStruct((blocks, columns, width), BF16),
            jax.ShapeDtypeStruct((owned, columns, width), F32),
        ],
        scratch_shapes=[
            pltpu.VMEM((half, kt, rows, width), BF16),
            pltpu.SemaphoreType.DMA((pieces,)),
            pltpu.VMEM(start_t.shape, F32),
            pltpu.SemaphoreType.DMA((coef_pieces,)),
            pltpu.SMEM(ids.shape, jnp.int32),
            pltpu.SemaphoreType.DMA(()),
        ],
        compiler_params=params(FIRST_LIMIT),
    )(ids, tiles, start_t)


def predict_half(ids, tiles, coef, other):
    row_blocks, kt, rows, width = tiles.shape
    columns = coef.shape[1]
    half = row_blocks // 2
    step = 16

    def kernel(ids_ref, tiles_ref, coef_ref, out_ref):
        base = side(other) * half

        @pl.loop(0, half // step)
        def _(i):
            for r in range(0, step, 2):
                at = i * step + r
                predict_pair(ids_ref, tiles_ref, coef_ref, out_ref, at, base + at, base + at, kt)

    return pl.pallas_call(
        kernel,
        in_specs=whole(2, 1),
        out_specs=whole(1, 0)[0],
        out_shape=jax.ShapeDtypeStruct((half, columns, rows), F32),
        compiler_params=params(),
    )(ids, tiles, coef)


def weigh(n_feat, live, parts, resp_t, copies):
    sources, count, columns, rows = parts.shape
    threshold = 1.4 * columns**0.5
    height = count * columns + PAD

    slots = resp_t.shape[0] // live.shape[1]

    def kernel(live_ref, parts_ref, resp_ref, out_ref):
        row, core, chip = place(n_feat)
        first = (core * (n_feat // 2) + chip) * count
        at = lax.broadcasted_iota(jnp.int32, live.shape, 0) == row
        at &= lax.broadcasted_iota(jnp.int32, live.shape, 1) == first // slots
        flag = jnp.sum(jnp.where(at, live_ref[...].astype(F32), 0.0), axis=0, keepdims=True)
        flag = jnp.sum(flag, axis=1, keepdims=True)
        lines = []
        for r in range(count):
            predicted = parts_ref[0, r].astype(F32)
            for s in range(1, sources):
                predicted = predicted + parts_ref[s, r].astype(F32)
            residual = resp_ref[first + r].astype(F32) - predicted
            norm = jnp.sqrt(jnp.sum(residual * residual, axis=0, keepdims=True))
            weight = flag * threshold / jnp.maximum(norm, threshold)
            scaled = (weight * residual).astype(BF16)
            for c in range(copies):
                out_ref[c, r * columns : (r + 1) * columns, :] = scaled
            lines.append(weight)
        lines.append(jnp.zeros((PAD - count, rows), F32))
        tail = jnp.concatenate(lines, axis=0).astype(BF16)
        for c in range(copies):
            out_ref[c, count * columns :, :] = tail

    return pl.pallas_call(
        kernel,
        in_specs=whole(3, 0),
        out_specs=whole(1, 0)[0],
        out_shape=jax.ShapeDtypeStruct((copies, height, rows), BF16),
        compiler_params=params(),
    )(live, parts, resp_t)


def gradient_half(ids, tiles, scaled, other, local_blocks, groups, before, keep_error):
    row_blocks, kt, rows, width = tiles.shape
    sources, height, _ = scaled.shape
    half = row_blocks // 2
    count = half // sources
    columns = (height - PAD) // count
    owned = local_blocks // groups
    n_before = len(before)
    turn = 2

    def kernel(ids_ref, tiles_ref, scaled_ref, *refs):
        grad, curv, *out = refs[n_before:]
        base = side(other) * half
        for ref in (grad, curv)[n_before:]:
            ref[...] = jnp.zeros_like(ref)

        def add(p):
            tail = scaled_ref[p, count * columns :, :].astype(F32)
            for r in range(count):
                row_block = base + p * count + r
                weights = jnp.broadcast_to(tail[r : r + 1, :], (rows, rows)).T
                placed = [tiles_ref[row_block, k] for k in range(kt)]
                sums = jnp.dot(
                    scaled_ref[p, r * columns : (r + 1) * columns, :],
                    jnp.concatenate(placed, axis=1),
                    preferred_element_type=F32,
                )
                for k in range(kt):
                    block = ids_ref[row_block * kt + k]
                    grad[block] += sums[:, k * width : (k + 1) * width]
                    wide = placed[k].astype(F32)
                    square = wide * wide * weights
                    curv[block] += jnp.sum(square.reshape(rows // 8, 8, width), axis=0)

        @pl.loop(0, sources // turn)
        def _(i):
            for t in range(turn):
                add(i * turn + t)

        if other:

            @pl.loop(0, groups)
            def _(g):
                lines = []
                for b in range(owned):
                    at = g * owned + b
                    rounded = grad[at].astype(BF16)
                    out[0][g, b * columns : (b + 1) * columns, :] = rounded
                    if keep_error:
                        grad[at] -= rounded.astype(F32)
                    lines.append(jnp.sum(curv[at], axis=0, keepdims=True))
                lines.append(jnp.zeros((PAD - owned, width), F32))
                out[0][g, owned * columns :, :] = jnp.concatenate(lines, axis=0).astype(BF16)

    out_shape = [
        jax.ShapeDtypeStruct((local_blocks, columns, width), F32),
        jax.ShapeDtypeStruct((local_blocks, 8, width), F32),
    ]
    if other:
        out_shape.append(jax.ShapeDtypeStruct((groups, owned * columns + PAD, width), BF16))
    return pl.pallas_call(
        kernel,
        in_specs=whole(2 + n_before, 1),
        out_specs=whole(len(out_shape), 0),
        out_shape=out_shape,
        input_output_aliases={3 + i: i for i in range(n_before)},
        compiler_params=params(),
    )(ids, tiles, scaled, *before)


def update(parts, exact, known, copies, owned):
    sources, height, width = parts.shape
    columns = (height - PAD) // owned
    shape = (owned, columns, width)
    first = known is None

    def kernel(parts_ref, exact_ref, *refs):
        sent_ref = refs[-1]

        def total(lo, hi):
            value = parts_ref[0, lo:hi, :].astype(F32)
            for s in range(1, sources):
                value = value + parts_ref[s, lo:hi, :].astype(F32)
            return value

        curvature = total(owned * columns, height)
        for b in range(owned):
            gradient = total(b * columns, (b + 1) * columns)
            coef = exact_ref[b]
            new = coef + STEP_SIZE * (gradient - RIDGE * coef) / (curvature[b : b + 1] + RIDGE)
            if first:
                refs[0][b] = new
            else:
                new = new - refs[0][0, b].astype(F32)
            for c in range(copies):
                sent_ref[c, b] = new.astype(BF16)

    out_shape = [jax.ShapeDtypeStruct((copies,) + shape, BF16)]
    if first:
        out_shape.insert(0, jax.ShapeDtypeStruct(shape, F32))
    return pl.pallas_call(
        kernel,
        in_specs=whole(2 + (not first), 0),
        out_specs=whole(len(out_shape), 0),
        out_shape=out_shape,
        compiler_params=params(),
    )(parts, exact, *(() if first else (known,)))


def finish(known, change):
    blocks, columns, width = known.shape
    pieces = 8
    step = blocks // pieces

    def kernel(known_ref, change_ref, out_hbm, held, sem):
        copies = []
        for p in range(pieces):
            for b in range(p * step, (p + 1) * step):
                held[:, b * width : (b + 1) * width] = known_ref[b].astype(F32) + change_ref[b].astype(F32)
            at = pl.ds(p * step * width, step * width)
            copies.append(pltpu.make_async_copy(held.at[:, at], out_hbm.at[:, at], sem.at[p]))
            copies[p].start()
        for copy in copies:
            copy.wait()

    shape = (columns, blocks * width)
    return pl.pallas_call(
        kernel,
        in_specs=whole(2, 0),
        out_specs=pl.BlockSpec(memory_space=pltpu.HBM),
        out_shape=jax.ShapeDtypeStruct(shape, F32),
        scratch_shapes=[pltpu.VMEM(shape, F32), pltpu.SemaphoreType.DMA((pieces,))],
        compiler_params=params(),
    )(known, change)


def make_body(n_row, n_feat):
    n_yz = n_feat // 2
    chips = [[2 * i + core for i in range(n_yz)] for core in range(2)]
    other_core = [(i, i ^ 1) for i in range(n_feat)]

    def swap_core(x):
        return lax.ppermute(x, "feat", other_core)

    def exchange_feat(x):
        return lax.all_to_all(x, "feat", 0, 0, axis_index_groups=chips, tiled=True)

    def exchange_row(x):
        return lax.all_to_all(x, "row", 0, 0, tiled=True)

    def body(design_tiles, block_ids, responses, live_groups, start_coef):
        row = lax.axis_index("row")
        feat = lax.axis_index("feat")
        _, owners, slots, kt, rows, width = design_tiles.shape
        row_blocks = owners * slots
        features, columns = start_coef.shape
        local_blocks = features // width
        tiles = design_tiles.reshape(row_blocks, kt, rows, width)
        resp_t = responses.reshape(row_blocks, rows, columns).swapaxes(1, 2)
        start_t = start_coef.T
        ids = lax.dynamic_index_in_dim(block_ids, row, 0, keepdims=False).reshape(-1)
        ids = (ids - feat * local_blocks).astype(jnp.int32)
        share = row_blocks // n_feat
        owned = local_blocks // n_row

        sent, carried = None, ()
        for iteration in range(ITERS):
            ends = iteration == ITERS - 1
            if iteration == 0:
                ahead, known, exact = predict_first(ids, tiles, start_t, owned)
            else:
                ahead = predict_half(ids, tiles, known, True)
            arrived = swap_core(ahead)
            kept = predict_half(ids, tiles, known, False)
            pair = (kept + arrived).astype(BF16)
            parts = exchange_feat(pair).reshape(n_yz, share, columns, rows)
            scaled = exchange_feat(weigh(n_feat, live_groups, parts, resp_t, n_yz))
            scaled_there = swap_core(scaled)
            before = gradient_half(
                ids, tiles, scaled, False, local_blocks, n_row, carried, False
            )
            error, _, partial = gradient_half(
                ids, tiles, scaled_there, True, local_blocks, n_row, before, not ends
            )
            carried = (error,)
            *new, sent = update(exchange_row(partial), exact, sent, n_row, owned)
            gathered = exchange_row(sent).reshape(local_blocks, columns, width)
            if ends:
                return finish(known, gathered).T
            known, exact = gathered, new[0]

    return body


def solution(mesh):
    in_specs = (
        P("row", None, None, "feat", None, None),
        P(None, None, None, "feat"),
        P("row", None, None, None, None),
        P(),
        P("feat", None),
    )
    return jax.shard_map(
        make_body(mesh.shape["row"], mesh.shape["feat"]),
        mesh=mesh,
        in_specs=in_specs,
        out_specs=P("feat", None),
        check_vma=False,
    )
```

```python
import jax
import jax.numpy as jnp
from jax import lax
from jax.experimental import pallas as pl
from jax.experimental.pallas import tpu as pltpu
from jax.sharding import PartitionSpec as P

ITERS = 2
STEP_SIZE = 0.25
RIDGE = 0.05
F32 = jnp.float32
BF16 = jnp.bfloat16
VMEM_LIMIT = 16 * 1024 * 1024
FIRST_LIMIT = 50 * 1024 * 1024

LANES = 128
PAD = 16


def params(limit=VMEM_LIMIT):
    return pltpu.CompilerParams(vmem_limit_bytes=limit)


def whole(count, scalars):
    smem = pl.BlockSpec(memory_space=pltpu.SMEM)
    vmem = pl.BlockSpec(memory_space=pltpu.VMEM)
    return [smem] * scalars + [vmem] * count


def place(n_feat):
    feat = lax.axis_index("feat")
    return lax.axis_index("row"), lax.rem(feat, 2), lax.div(feat, 2)


def side(other):
    core = lax.axis_index("feat") % 2
    return 1 - core if other else core


def blocks_of(ids_ref, other, kt):
    line = ids_ref[pl.ds(side(other), 1), :]
    return lambda row_block, k: line[0, row_block * kt + k]


def predict_pair(block_of, tiles_ref, coef_ref, out_ref, put, at, kt):
    picked, placed = [], []
    for r in range(2):
        picked.append(jnp.concatenate([coef_ref[block_of(put + r, k)] for k in range(kt)], axis=1))
        placed.append(jnp.concatenate([tiles_ref[at + r, k] for k in range(kt)], axis=1))
    both = lax.dot_general(
        jnp.concatenate(picked, axis=0),
        jnp.concatenate(placed, axis=0),
        (((1,), (1,)), ((), ())),
        preferred_element_type=F32,
    )
    columns, rows = picked[0].shape[0], placed[0].shape[0]
    out_ref[put] = both[:columns, :rows]
    out_ref[put + 1] = both[columns:, rows:]


def predict_first(ids, tiles, start_t, owned):
    row_blocks, kt, rows, width = tiles.shape
    columns, features = start_t.shape
    blocks = features // width
    half = row_blocks // 2
    step = 8
    pieces = half // step
    coef_pieces = 4
    share = features // coef_pieces

    def kernel(ids_ref, tiles_hbm, start_hbm, out_ref, coef_ref, own_ref, *scratch):
        held, tile_sem, start_ref, start_sem = scratch
        base = side(True) * half
        block_of = blocks_of(ids_ref, True, kt)
        starts, copies = [], []
        for p in range(coef_pieces):
            at = pl.ds(p * share, share)
            starts.append(
                pltpu.make_async_copy(start_hbm.at[:, at], start_ref.at[:, at], start_sem.at[p])
            )
        for p in range(pieces):
            copies.append(
                pltpu.make_async_copy(
                    tiles_hbm.at[pl.ds(base + p * step, step)],
                    held.at[pl.ds(p * step, step)],
                    tile_sem.at[p],
                )
            )
        for copy in starts + copies:
            copy.start()
        for p in range(coef_pieces):
            starts[p].wait()
            for b in range(p * blocks // coef_pieces, (p + 1) * blocks // coef_pieces):
                coef_ref[b] = start_ref[:, b * width : (b + 1) * width].astype(BF16)
        for b in range(owned):
            at = pl.multiple_of((lax.axis_index("row") * owned + b) * width, width)
            own_ref[b] = start_ref[:, pl.ds(at, width)]
        for p in range(pieces):
            copies[p].wait()
            for r in range(0, step, 2):
                at = p * step + r
                predict_pair(block_of, held, coef_ref, out_ref, at, at, kt)

    hbm = pl.BlockSpec(memory_space=pltpu.HBM)
    return pl.pallas_call(
        kernel,
        in_specs=whole(1, 0) + [hbm, hbm],
        out_specs=whole(3, 0),
        out_shape=[
            jax.ShapeDtypeStruct((half, columns, rows), F32),
            jax.ShapeDtypeStruct((blocks, columns, width), BF16),
            jax.ShapeDtypeStruct((owned, columns, width), F32),
        ],
        scratch_shapes=[
            pltpu.VMEM((half, kt, rows, width), BF16),
            pltpu.SemaphoreType.DMA((pieces,)),
            pltpu.VMEM(start_t.shape, F32),
            pltpu.SemaphoreType.DMA((coef_pieces,)),
        ],
        compiler_params=params(FIRST_LIMIT),
    )(ids, tiles, start_t)


def predict_half(ids, tiles, coef, other):
    row_blocks, kt, rows, width = tiles.shape
    columns = coef.shape[1]
    half = row_blocks // 2

    def kernel(ids_ref, tiles_ref, coef_ref, out_ref):
        base = side(other) * half
        block_of = blocks_of(ids_ref, other, kt)
        for r in range(0, half, 2):
            predict_pair(block_of, tiles_ref, coef_ref, out_ref, r, base + r, kt)

    return pl.pallas_call(
        kernel,
        in_specs=whole(3, 0),
        out_specs=whole(1, 0)[0],
        out_shape=jax.ShapeDtypeStruct((half, columns, rows), F32),
        compiler_params=params(),
    )(ids, tiles, coef)


def weigh(n_feat, live, parts, resp_t, copies):
    sources, count, columns, rows = parts.shape
    threshold = 1.4 * columns**0.5
    height = count * columns + PAD

    slots = resp_t.shape[0] // live.shape[1]

    def kernel(live_ref, parts_ref, resp_ref, out_ref):
        row, core, chip = place(n_feat)
        first = (core * (n_feat // 2) + chip) * count
        at = lax.broadcasted_iota(jnp.int32, live.shape, 0) == row
        at &= lax.broadcasted_iota(jnp.int32, live.shape, 1) == first // slots
        flag = jnp.sum(jnp.where(at, live_ref[...].astype(F32), 0.0), axis=0, keepdims=True)
        flag = jnp.sum(flag, axis=1, keepdims=True)
        lines = []
        for r in range(count):
            predicted = parts_ref[0, r].astype(F32)
            for s in range(1, sources):
                predicted = predicted + parts_ref[s, r].astype(F32)
            residual = resp_ref[first + r].astype(F32) - predicted
            norm = jnp.sqrt(jnp.sum(residual * residual, axis=0, keepdims=True))
            weight = flag * threshold / jnp.maximum(norm, threshold)
            scaled = (weight * residual).astype(BF16)
            for c in range(copies):
                out_ref[c, r * columns : (r + 1) * columns, :] = scaled
            lines.append(weight)
        lines.append(jnp.zeros((PAD - count, rows), F32))
        tail = jnp.concatenate(lines, axis=0).astype(BF16)
        for c in range(copies):
            out_ref[c, count * columns :, :] = tail

    return pl.pallas_call(
        kernel,
        in_specs=whole(3, 0),
        out_specs=whole(1, 0)[0],
        out_shape=jax.ShapeDtypeStruct((copies, height, rows), BF16),
        compiler_params=params(),
    )(live, parts, resp_t)


def gradient_half(ids, tiles, scaled, other, local_blocks, groups, before, keep_error):
    row_blocks, kt, rows, width = tiles.shape
    sources, height, _ = scaled.shape
    half = row_blocks // 2
    count = half // sources
    columns = (height - PAD) // count
    owned = local_blocks // groups
    n_before = len(before)

    def kernel(ids_ref, tiles_ref, scaled_ref, *refs):
        grad, curv, *out = refs[n_before:]
        base = side(other) * half
        block_of = blocks_of(ids_ref, other, kt)
        for ref in (grad, curv)[n_before:]:
            ref[...] = jnp.zeros_like(ref)

        def add(p):
            tail = scaled_ref[p, count * columns :, :].astype(F32)
            for r in range(count):
                row_block = base + p * count + r
                weights = jnp.broadcast_to(tail[r : r + 1, :], (rows, rows)).T
                placed = [tiles_ref[row_block, k] for k in range(kt)]
                sums = jnp.dot(
                    scaled_ref[p, r * columns : (r + 1) * columns, :],
                    jnp.concatenate(placed, axis=1),
                    preferred_element_type=F32,
                )
                for k in range(kt):
                    block = block_of(p * count + r, k)
                    grad[block] += sums[:, k * width : (k + 1) * width]
                    wide = placed[k].astype(F32)
                    square = wide * wide * weights
                    curv[block] += jnp.sum(square.reshape(rows // 8, 8, width), axis=0)

        for p in range(sources):
            add(p)

        if other:

            @pl.loop(0, groups)
            def _(g):
                lines = []
                for b in range(owned):
                    at = g * owned + b
                    rounded = grad[at].astype(BF16)
                    out[0][g, b * columns : (b + 1) * columns, :] = rounded
                    if keep_error:
                        grad[at] -= rounded.astype(F32)
                    lines.append(jnp.sum(curv[at], axis=0, keepdims=True))
                lines.append(jnp.zeros((PAD - owned, width), F32))
                out[0][g, owned * columns :, :] = jnp.concatenate(lines, axis=0).astype(BF16)

    out_shape = [
        jax.ShapeDtypeStruct((local_blocks, columns, width), F32),
        jax.ShapeDtypeStruct((local_blocks, 8, width), F32),
    ]
    if other:
        out_shape.append(jax.ShapeDtypeStruct((groups, owned * columns + PAD, width), BF16))
    return pl.pallas_call(
        kernel,
        in_specs=whole(3 + n_before, 0),
        out_specs=whole(len(out_shape), 0),
        out_shape=out_shape,
        input_output_aliases={3 + i: i for i in range(n_before)},
        compiler_params=params(),
    )(ids, tiles, scaled, *before)


def update(parts, exact, known, copies, owned):
    sources, height, width = parts.shape
    columns = (height - PAD) // owned
    shape = (owned, columns, width)
    first = known is None

    def kernel(parts_ref, exact_ref, *refs):
        sent_ref = refs[-1]

        def total(lo, hi):
            value = parts_ref[0, lo:hi, :].astype(F32)
            for s in range(1, sources):
                value = value + parts_ref[s, lo:hi, :].astype(F32)
            return value

        curvature = total(owned * columns, height)
        for b in range(owned):
            gradient = total(b * columns, (b + 1) * columns)
            coef = exact_ref[b]
            new = coef + STEP_SIZE * (gradient - RIDGE * coef) / (curvature[b : b + 1] + RIDGE)
            if first:
                refs[0][b] = new
            else:
                new = new - refs[0][0, b].astype(F32)
            for c in range(copies):
                sent_ref[c, b] = new.astype(BF16)

    out_shape = [jax.ShapeDtypeStruct((copies,) + shape, BF16)]
    if first:
        out_shape.insert(0, jax.ShapeDtypeStruct(shape, F32))
    return pl.pallas_call(
        kernel,
        in_specs=whole(2 + (not first), 0),
        out_specs=whole(len(out_shape), 0),
        out_shape=out_shape,
        compiler_params=params(),
    )(parts, exact, *(() if first else (known,)))


def finish(known, change):
    blocks, columns, width = known.shape
    pieces = 8
    step = blocks // pieces

    def kernel(known_ref, change_ref, out_hbm, held, sem):
        copies = []
        for p in range(pieces):
            for b in range(p * step, (p + 1) * step):
                held[:, b * width : (b + 1) * width] = known_ref[b].astype(F32) + change_ref[b].astype(F32)
            at = pl.ds(p * step * width, step * width)
            copies.append(pltpu.make_async_copy(held.at[:, at], out_hbm.at[:, at], sem.at[p]))
            copies[p].start()
        for copy in copies:
            copy.wait()

    shape = (columns, blocks * width)
    return pl.pallas_call(
        kernel,
        in_specs=whole(2, 0),
        out_specs=pl.BlockSpec(memory_space=pltpu.HBM),
        out_shape=jax.ShapeDtypeStruct(shape, F32),
        scratch_shapes=[pltpu.VMEM(shape, F32), pltpu.SemaphoreType.DMA((pieces,))],
        compiler_params=params(),
    )(known, change)


def make_body(n_row, n_feat):
    n_yz = n_feat // 2
    chips = [[2 * i + core for i in range(n_yz)] for core in range(2)]
    other_core = [(i, i ^ 1) for i in range(n_feat)]

    def swap_core(x):
        return lax.ppermute(x, "feat", other_core)

    def exchange_feat(x):
        return lax.all_to_all(x, "feat", 0, 0, axis_index_groups=chips, tiled=True)

    def exchange_row(x):
        return lax.all_to_all(x, "row", 0, 0, tiled=True)

    def body(design_tiles, block_ids, responses, live_groups, start_coef):
        row = lax.axis_index("row")
        feat = lax.axis_index("feat")
        _, owners, slots, kt, rows, width = design_tiles.shape
        row_blocks = owners * slots
        features, columns = start_coef.shape
        local_blocks = features // width
        tiles = design_tiles.reshape(row_blocks, kt, rows, width)
        resp_t = responses.reshape(row_blocks, rows, columns).swapaxes(1, 2)
        start_t = start_coef.T
        ids = lax.dynamic_index_in_dim(block_ids, row, 0, keepdims=False).reshape(-1)
        ids = (ids - feat * local_blocks).astype(jnp.int32).reshape(2, -1)
        ids = jnp.pad(ids, ((0, 0), (0, -ids.shape[1] % LANES)))
        share = row_blocks // n_feat
        owned = local_blocks // n_row

        sent, carried = None, ()
        for iteration in range(ITERS):
            ends = iteration == ITERS - 1
            if iteration == 0:
                ahead, known, exact = predict_first(ids, tiles, start_t, owned)
            else:
                ahead = predict_half(ids, tiles, known, True)
            arrived = swap_core(ahead)
            kept = predict_half(ids, tiles, known, False)
            pair = (kept + arrived).astype(BF16)
            parts = exchange_feat(pair).reshape(n_yz, share, columns, rows)
            scaled = exchange_feat(weigh(n_feat, live_groups, parts, resp_t, n_yz))
            scaled_there = swap_core(scaled)
            before = gradient_half(
                ids, tiles, scaled, False, local_blocks, n_row, carried, False
            )
            error, _, partial = gradient_half(
                ids, tiles, scaled_there, True, local_blocks, n_row, before, not ends
            )
            carried = (error,)
            *new, sent = update(exchange_row(partial), exact, sent, n_row, owned)
            gathered = exchange_row(sent).reshape(local_blocks, columns, width)
            if ends:
                return finish(known, gathered).T
            known, exact = gathered, new[0]

    return body


def solution(mesh):
    in_specs = (
        P("row", None, None, "feat", None, None),
        P(None, None, None, "feat"),
        P("row", None, None, None, None),
        P(),
        P("feat", None),
    )
    return jax.shard_map(
        make_body(mesh.shape["row"], mesh.shape["feat"]),
        mesh=mesh,
        in_specs=in_specs,
        out_specs=P("feat", None),
        check_vma=False,
    )
```

```python
import jax
import jax.numpy as jnp
from jax import lax
from jax.experimental import pallas as pl
from jax.experimental.pallas import tpu as pltpu
from jax.sharding import PartitionSpec as P

ITERS = 2
STEP_SIZE = 0.25
RIDGE = 0.05
F32 = jnp.float32
BF16 = jnp.bfloat16
VMEM_LIMIT = 16 * 1024 * 1024
FIRST_LIMIT = 51 * 1024 * 1024

LANES = 128
PAD = 16


def params(limit=VMEM_LIMIT):
    return pltpu.CompilerParams(vmem_limit_bytes=limit)


def whole(count, scalars):
    smem = pl.BlockSpec(memory_space=pltpu.SMEM)
    vmem = pl.BlockSpec(memory_space=pltpu.VMEM)
    return [smem] * scalars + [vmem] * count


def place(n_feat):
    feat = lax.axis_index("feat")
    return lax.axis_index("row"), lax.rem(feat, 2), lax.div(feat, 2)


def side(other):
    core = lax.axis_index("feat") % 2
    return 1 - core if other else core


def blocks_of(ids_ref, other, kt):
    line = ids_ref[pl.ds(side(other), 1), :]
    return lambda row_block, k: line[0, row_block * kt + k]


def predict_pair(block_of, tiles_ref, coef_ref, out_ref, put, at, kt):
    picked, placed = [], []
    for r in range(2):
        picked.append(jnp.concatenate([coef_ref[block_of(put + r, k)] for k in range(kt)], axis=1))
        placed.append(jnp.concatenate([tiles_ref[at + r, k] for k in range(kt)], axis=1))
    both = lax.dot_general(
        jnp.concatenate(picked, axis=0),
        jnp.concatenate(placed, axis=0),
        (((1,), (1,)), ((), ())),
        preferred_element_type=F32,
    )
    columns, rows = picked[0].shape[0], placed[0].shape[0]
    out_ref[put] = both[:columns, :rows].astype(out_ref.dtype)
    out_ref[put + 1] = both[columns:, rows:].astype(out_ref.dtype)


def predict_first(ids, tiles, start_t, owned, dtype):
    row_blocks, kt, rows, width = tiles.shape
    columns, features = start_t.shape
    blocks = features // width
    half = row_blocks // 2
    step = 8
    pieces = half // step
    coef_pieces = 4
    share = features // coef_pieces

    def kernel(ids_vmem, tiles_hbm, start_hbm, out_ref, coef_ref, own_ref, *scratch):
        held, tile_sem, start_ref, start_sem, ids_ref, ids_sem = scratch
        other = side(True)
        base = other * half
        block_of = lambda row_block, k: ids_ref[other, row_block * kt + k]
        ids_copy = pltpu.make_async_copy(ids_vmem, ids_ref, ids_sem)
        starts, copies = [], []
        for p in range(coef_pieces):
            at = pl.ds(p * share, share)
            starts.append(
                pltpu.make_async_copy(start_hbm.at[:, at], start_ref.at[:, at], start_sem.at[p])
            )
        for p in range(pieces):
            copies.append(
                pltpu.make_async_copy(
                    tiles_hbm.at[pl.ds(base + p * step, step)],
                    held.at[pl.ds(p * step, step)],
                    tile_sem.at[p],
                )
            )
        for copy in starts + [ids_copy] + copies:
            copy.start()
        for p in range(coef_pieces):
            starts[p].wait()
            for b in range(p * blocks // coef_pieces, (p + 1) * blocks // coef_pieces):
                coef_ref[b] = start_ref[:, b * width : (b + 1) * width].astype(BF16)
        for b in range(owned):
            at = pl.multiple_of((lax.axis_index("row") * owned + b) * width, width)
            own_ref[b] = start_ref[:, pl.ds(at, width)]
        ids_copy.wait()
        for p in range(pieces):
            copies[p].wait()
            for r in range(0, step, 2):
                at = p * step + r
                predict_pair(block_of, held, coef_ref, out_ref, at, at, kt)

    hbm = pl.BlockSpec(memory_space=pltpu.HBM)
    return pl.pallas_call(
        kernel,
        in_specs=whole(1, 0) + [hbm, hbm],
        out_specs=whole(3, 0),
        out_shape=[
            jax.ShapeDtypeStruct((half, columns, rows), dtype),
            jax.ShapeDtypeStruct((blocks, columns, width), BF16),
            jax.ShapeDtypeStruct((owned, columns, width), F32),
        ],
        scratch_shapes=[
            pltpu.VMEM((half, kt, rows, width), BF16),
            pltpu.SemaphoreType.DMA((pieces,)),
            pltpu.VMEM(start_t.shape, F32),
            pltpu.SemaphoreType.DMA((coef_pieces,)),
            pltpu.SMEM(ids.shape, jnp.int32),
            pltpu.SemaphoreType.DMA(()),
        ],
        compiler_params=params(FIRST_LIMIT),
    )(ids, tiles, start_t)


def predict_half(ids, tiles, coef, other):
    row_blocks, kt, rows, width = tiles.shape
    columns = coef.shape[1]
    half = row_blocks // 2

    def kernel(ids_ref, tiles_ref, coef_ref, out_ref):
        base = side(other) * half
        block_of = blocks_of(ids_ref, other, kt)
        for r in range(0, half, 2):
            predict_pair(block_of, tiles_ref, coef_ref, out_ref, r, base + r, kt)

    return pl.pallas_call(
        kernel,
        in_specs=whole(3, 0),
        out_specs=whole(1, 0)[0],
        out_shape=jax.ShapeDtypeStruct((half, columns, rows), F32),
        compiler_params=params(),
    )(ids, tiles, coef)


def weigh(n_feat, live, parts, resp_t, copies):
    sources, count, columns, rows = parts.shape
    threshold = 1.4 * columns**0.5
    height = count * columns + PAD

    slots = resp_t.shape[0] // live.shape[1]

    def kernel(live_ref, parts_ref, resp_ref, out_ref):
        row, core, chip = place(n_feat)
        first = (core * (n_feat // 2) + chip) * count
        at = lax.broadcasted_iota(jnp.int32, live.shape, 0) == row
        at &= lax.broadcasted_iota(jnp.int32, live.shape, 1) == first // slots
        flag = jnp.sum(jnp.where(at, live_ref[...].astype(F32), 0.0), axis=0, keepdims=True)
        flag = jnp.sum(flag, axis=1, keepdims=True)
        lines = []
        for r in range(count):
            predicted = parts_ref[0, r].astype(F32)
            for s in range(1, sources):
                predicted = predicted + parts_ref[s, r].astype(F32)
            residual = resp_ref[first + r].astype(F32) - predicted
            norm = jnp.sqrt(jnp.sum(residual * residual, axis=0, keepdims=True))
            weight = flag * threshold / jnp.maximum(norm, threshold)
            scaled = (weight * residual).astype(BF16)
            for c in range(copies):
                out_ref[c, r * columns : (r + 1) * columns, :] = scaled
            lines.append(weight)
        lines.append(jnp.zeros((PAD - count, rows), F32))
        tail = jnp.concatenate(lines, axis=0).astype(BF16)
        for c in range(copies):
            out_ref[c, count * columns :, :] = tail

    return pl.pallas_call(
        kernel,
        in_specs=whole(3, 0),
        out_specs=whole(1, 0)[0],
        out_shape=jax.ShapeDtypeStruct((copies, height, rows), BF16),
        compiler_params=params(),
    )(live, parts, resp_t)


def gradient_half(ids, tiles, scaled, other, local_blocks, groups, before, keep_error):
    row_blocks, kt, rows, width = tiles.shape
    sources, height, _ = scaled.shape
    half = row_blocks // 2
    count = half // sources
    columns = (height - PAD) // count
    owned = local_blocks // groups
    n_before = len(before)

    def kernel(ids_ref, tiles_ref, scaled_ref, *refs):
        grad, curv, *out = refs[n_before:]
        base = side(other) * half
        block_of = blocks_of(ids_ref, other, kt)
        for ref in (grad, curv)[n_before:]:
            ref[...] = jnp.zeros_like(ref)

        def add(p):
            tail = scaled_ref[p, count * columns :, :].astype(F32)
            for r in range(count):
                row_block = base + p * count + r
                weights = jnp.broadcast_to(tail[r : r + 1, :], (rows, rows)).T
                placed = [tiles_ref[row_block, k] for k in range(kt)]
                sums = jnp.dot(
                    scaled_ref[p, r * columns : (r + 1) * columns, :],
                    jnp.concatenate(placed, axis=1),
                    preferred_element_type=F32,
                )
                for k in range(kt):
                    block = block_of(p * count + r, k)
                    grad[block] += sums[:, k * width : (k + 1) * width]
                    wide = placed[k].astype(F32)
                    square = wide * wide * weights
                    curv[block] += jnp.sum(square.reshape(rows // 8, 8, width), axis=0)

        for p in range(sources):
            add(p)

        if other:

            @pl.loop(0, groups)
            def _(g):
                lines = []
                for b in range(owned):
                    at = g * owned + b
                    rounded = grad[at].astype(BF16)
                    out[0][g, b * columns : (b + 1) * columns, :] = rounded
                    if keep_error:
                        grad[at] -= rounded.astype(F32)
                    lines.append(jnp.sum(curv[at], axis=0, keepdims=True))
                lines.append(jnp.zeros((PAD - owned, width), F32))
                out[0][g, owned * columns :, :] = jnp.concatenate(lines, axis=0).astype(BF16)

    out_shape = [
        jax.ShapeDtypeStruct((local_blocks, columns, width), F32),
        jax.ShapeDtypeStruct((local_blocks, 8, width), F32),
    ]
    if other:
        out_shape.append(jax.ShapeDtypeStruct((groups, owned * columns + PAD, width), BF16))
    return pl.pallas_call(
        kernel,
        in_specs=whole(3 + n_before, 0),
        out_specs=whole(len(out_shape), 0),
        out_shape=out_shape,
        input_output_aliases={3 + i: i for i in range(n_before)},
        compiler_params=params(),
    )(ids, tiles, scaled, *before)


def update(parts, exact, known, copies, owned):
    sources, height, width = parts.shape
    columns = (height - PAD) // owned
    shape = (owned, columns, width)
    first = known is None

    def kernel(parts_ref, exact_ref, *refs):
        sent_ref = refs[-1]

        def total(lo, hi):
            value = parts_ref[0, lo:hi, :].astype(F32)
            for s in range(1, sources):
                value = value + parts_ref[s, lo:hi, :].astype(F32)
            return value

        curvature = total(owned * columns, height)
        for b in range(owned):
            gradient = total(b * columns, (b + 1) * columns)
            coef = exact_ref[b]
            new = coef + STEP_SIZE * (gradient - RIDGE * coef) / (curvature[b : b + 1] + RIDGE)
            if first:
                refs[0][b] = new
            else:
                new = new - refs[0][0, b].astype(F32)
            for c in range(copies):
                sent_ref[c, b] = new.astype(BF16)

    out_shape = [jax.ShapeDtypeStruct((copies,) + shape, BF16)]
    if first:
        out_shape.insert(0, jax.ShapeDtypeStruct(shape, F32))
    return pl.pallas_call(
        kernel,
        in_specs=whole(2 + (not first), 0),
        out_specs=whole(len(out_shape), 0),
        out_shape=out_shape,
        compiler_params=params(),
    )(parts, exact, *(() if first else (known,)))


def finish(known, change):
    blocks, columns, width = known.shape
    pieces = 8
    step = blocks // pieces

    def kernel(known_ref, change_ref, out_hbm, held, sem):
        copies = []
        for p in range(pieces):
            for b in range(p * step, (p + 1) * step):
                held[:, b * width : (b + 1) * width] = known_ref[b].astype(F32) + change_ref[b].astype(F32)
            at = pl.ds(p * step * width, step * width)
            copies.append(pltpu.make_async_copy(held.at[:, at], out_hbm.at[:, at], sem.at[p]))
            copies[p].start()
        for copy in copies:
            copy.wait()

    shape = (columns, blocks * width)
    return pl.pallas_call(
        kernel,
        in_specs=whole(2, 0),
        out_specs=pl.BlockSpec(memory_space=pltpu.HBM),
        out_shape=jax.ShapeDtypeStruct(shape, F32),
        scratch_shapes=[pltpu.VMEM(shape, F32), pltpu.SemaphoreType.DMA((pieces,))],
        compiler_params=params(),
    )(known, change)


def make_body(n_row, n_feat):
    n_yz = n_feat // 2
    chips = [[2 * i + core for i in range(n_yz)] for core in range(2)]
    other_core = [(i, i ^ 1) for i in range(n_feat)]

    def swap_core(x):
        return lax.ppermute(x, "feat", other_core)

    def exchange_feat(x):
        return lax.all_to_all(x, "feat", 0, 0, axis_index_groups=chips, tiled=True)

    def exchange_row(x):
        return lax.all_to_all(x, "row", 0, 0, tiled=True)

    def body(design_tiles, block_ids, responses, live_groups, start_coef):
        row = lax.axis_index("row")
        feat = lax.axis_index("feat")
        _, owners, slots, kt, rows, width = design_tiles.shape
        row_blocks = owners * slots
        features, columns = start_coef.shape
        local_blocks = features // width
        tiles = design_tiles.reshape(row_blocks, kt, rows, width)
        resp_t = responses.reshape(row_blocks, rows, columns).swapaxes(1, 2)
        start_t = start_coef.T
        ids = lax.dynamic_index_in_dim(block_ids, row, 0, keepdims=False).reshape(-1)
        ids = (ids - feat * local_blocks).astype(jnp.int32).reshape(2, -1)
        ids = jnp.pad(ids, ((0, 0), (0, -ids.shape[1] % LANES)))
        share = row_blocks // n_feat
        owned = local_blocks // n_row

        sent, carried = None, ()
        for iteration in range(ITERS):
            ends = iteration == ITERS - 1
            if iteration == 0:
                ahead, known, exact = predict_first(ids, tiles, start_t, owned, BF16)
            else:
                ahead = predict_half(ids, tiles, known, True)
            arrived = swap_core(ahead)
            kept = predict_half(ids, tiles, known, False)
            pair = (kept + arrived.astype(F32)).astype(BF16)
            parts = exchange_feat(pair).reshape(n_yz, share, columns, rows)
            scaled = exchange_feat(weigh(n_feat, live_groups, parts, resp_t, n_yz))
            scaled_there = swap_core(scaled)
            before = gradient_half(
                ids, tiles, scaled, False, local_blocks, n_row, carried, False
            )
            error, _, partial = gradient_half(
                ids, tiles, scaled_there, True, local_blocks, n_row, before, not ends
            )
            carried = (error,)
            *new, sent = update(exchange_row(partial), exact, sent, n_row, owned)
            gathered = exchange_row(sent).reshape(local_blocks, columns, width)
            if ends:
                return finish(known, gathered).T
            known, exact = gathered, new[0]

    return body


def solution(mesh):
    in_specs = (
        P("row", None, None, "feat", None, None),
        P(None, None, None, "feat"),
        P("row", None, None, None, None),
        P(),
        P("feat", None),
    )
    return jax.shard_map(
        make_body(mesh.shape["row"], mesh.shape["feat"]),
        mesh=mesh,
        in_specs=in_specs,
        out_specs=P("feat", None),
        check_vma=False,
    )
```

```python
import jax
import jax.numpy as jnp
from jax import lax
from jax.experimental import pallas as pl
from jax.experimental.pallas import tpu as pltpu
from jax.sharding import PartitionSpec as P

ITERS = 2
STEP_SIZE = 0.25
RIDGE = 0.05
F32 = jnp.float32
BF16 = jnp.bfloat16
VMEM_LIMIT = 16 * 1024 * 1024
FIRST_LIMIT = 51 * 1024 * 1024

LANES = 128
PAD = 16


def params(limit=VMEM_LIMIT):
    return pltpu.CompilerParams(vmem_limit_bytes=limit)


def whole(count, scalars):
    smem = pl.BlockSpec(memory_space=pltpu.SMEM)
    vmem = pl.BlockSpec(memory_space=pltpu.VMEM)
    return [smem] * scalars + [vmem] * count


def place(n_feat):
    feat = lax.axis_index("feat")
    return lax.axis_index("row"), lax.rem(feat, 2), lax.div(feat, 2)


def side(other):
    core = lax.axis_index("feat") % 2
    return 1 - core if other else core


def blocks_of(ids_ref, other, kt):
    line = ids_ref[pl.ds(side(other), 1), :]
    return lambda row_block, k: line[0, row_block * kt + k]


def predict_pair(block_of, tiles_ref, coef_ref, out_ref, put, at, kt):
    picked, placed = [], []
    for r in range(2):
        picked.append(jnp.concatenate([coef_ref[block_of(put + r, k)] for k in range(kt)], axis=1))
        placed.append(jnp.concatenate([tiles_ref[at + r, k] for k in range(kt)], axis=1))
    both = lax.dot_general(
        jnp.concatenate(picked, axis=0),
        jnp.concatenate(placed, axis=0),
        (((1,), (1,)), ((), ())),
        preferred_element_type=F32,
    )
    columns, rows = picked[0].shape[0], placed[0].shape[0]
    out_ref[put] = both[:columns, :rows].astype(out_ref.dtype)
    out_ref[put + 1] = both[columns:, rows:].astype(out_ref.dtype)


def predict_first(ids, tiles, start_t, owned, dtype):
    row_blocks, kt, rows, width = tiles.shape
    columns, features = start_t.shape
    blocks = features // width
    half = row_blocks // 2
    step = 8
    pieces = half // step
    coef_pieces = 4
    share = features // coef_pieces

    def kernel(ids_vmem, tiles_hbm, start_hbm, out_ref, coef_ref, own_ref, *scratch):
        held, tile_sem, start_ref, start_sem, ids_ref, ids_sem = scratch
        other = side(True)
        base = other * half
        block_of = lambda row_block, k: ids_ref[other, row_block * kt + k]
        ids_copy = pltpu.make_async_copy(ids_vmem, ids_ref, ids_sem)
        starts, copies = [], []
        for p in range(coef_pieces):
            at = pl.ds(p * share, share)
            starts.append(
                pltpu.make_async_copy(start_hbm.at[:, at], start_ref.at[:, at], start_sem.at[p])
            )
        for p in range(pieces):
            copies.append(
                pltpu.make_async_copy(
                    tiles_hbm.at[pl.ds(base + p * step, step)],
                    held.at[pl.ds(p * step, step)],
                    tile_sem.at[p],
                )
            )
        for copy in starts + [ids_copy] + copies:
            copy.start()
        for p in range(coef_pieces):
            starts[p].wait()
            for b in range(p * blocks // coef_pieces, (p + 1) * blocks // coef_pieces):
                coef_ref[b] = start_ref[:, b * width : (b + 1) * width].astype(BF16)
        for b in range(owned):
            at = pl.multiple_of((lax.axis_index("row") * owned + b) * width, width)
            own_ref[b] = start_ref[:, pl.ds(at, width)]
        ids_copy.wait()
        for p in range(pieces):
            copies[p].wait()
            for r in range(0, step, 2):
                at = p * step + r
                predict_pair(block_of, held, coef_ref, out_ref, at, at, kt)

    hbm = pl.BlockSpec(memory_space=pltpu.HBM)
    return pl.pallas_call(
        kernel,
        in_specs=whole(1, 0) + [hbm, hbm],
        out_specs=whole(3, 0),
        out_shape=[
            jax.ShapeDtypeStruct((half, columns, rows), dtype),
            jax.ShapeDtypeStruct((blocks, columns, width), BF16),
            jax.ShapeDtypeStruct((owned, columns, width), F32),
        ],
        scratch_shapes=[
            pltpu.VMEM((half, kt, rows, width), BF16),
            pltpu.SemaphoreType.DMA((pieces,)),
            pltpu.VMEM(start_t.shape, F32),
            pltpu.SemaphoreType.DMA((coef_pieces,)),
            pltpu.SMEM(ids.shape, jnp.int32),
            pltpu.SemaphoreType.DMA(()),
        ],
        compiler_params=params(FIRST_LIMIT),
    )(ids, tiles, start_t)


def predict_half(ids, tiles, coef, other):
    row_blocks, kt, rows, width = tiles.shape
    columns = coef.shape[1]
    half = row_blocks // 2

    def kernel(ids_ref, tiles_ref, coef_ref, out_ref):
        base = side(other) * half
        block_of = blocks_of(ids_ref, other, kt)
        for r in range(0, half, 2):
            predict_pair(block_of, tiles_ref, coef_ref, out_ref, r, base + r, kt)

    return pl.pallas_call(
        kernel,
        in_specs=whole(3, 0),
        out_specs=whole(1, 0)[0],
        out_shape=jax.ShapeDtypeStruct((half, columns, rows), F32),
        compiler_params=params(),
    )(ids, tiles, coef)


def weigh(n_feat, live, parts, resp_t, copies):
    sources, count, columns, rows = parts.shape
    threshold = 1.4 * columns**0.5
    height = count * columns + PAD

    slots = resp_t.shape[0] // live.shape[1]

    def kernel(live_ref, parts_ref, resp_ref, out_ref):
        row, core, chip = place(n_feat)
        first = (core * (n_feat // 2) + chip) * count
        at = lax.broadcasted_iota(jnp.int32, live.shape, 0) == row
        at &= lax.broadcasted_iota(jnp.int32, live.shape, 1) == first // slots
        flag = jnp.sum(jnp.where(at, live_ref[...].astype(F32), 0.0), axis=0, keepdims=True)
        flag = jnp.sum(flag, axis=1, keepdims=True)
        lines = []
        for r in range(count):
            predicted = parts_ref[0, r].astype(F32)
            for s in range(1, sources):
                predicted = predicted + parts_ref[s, r].astype(F32)
            residual = resp_ref[first + r].astype(F32) - predicted
            norm = jnp.sqrt(jnp.sum(residual * residual, axis=0, keepdims=True))
            weight = flag * threshold / jnp.maximum(norm, threshold)
            scaled = (weight * residual).astype(BF16)
            for c in range(copies):
                out_ref[c, r * columns : (r + 1) * columns, :] = scaled
            lines.append(weight)
        lines.append(jnp.zeros((PAD - count, rows), F32))
        tail = jnp.concatenate(lines, axis=0).astype(BF16)
        for c in range(copies):
            out_ref[c, count * columns :, :] = tail

    return pl.pallas_call(
        kernel,
        in_specs=whole(3, 0),
        out_specs=whole(1, 0)[0],
        out_shape=jax.ShapeDtypeStruct((copies, height, rows), BF16),
        compiler_params=params(),
    )(live, parts, resp_t)


def gradient_half(ids, tiles, scaled, other, local_blocks, groups, before, keep_error):
    row_blocks, kt, rows, width = tiles.shape
    sources, height, _ = scaled.shape
    half = row_blocks // 2
    count = half // sources
    columns = (height - PAD) // count
    owned = local_blocks // groups
    n_before = len(before)

    def kernel(ids_ref, tiles_ref, scaled_ref, *refs):
        grad, curv, *out = refs[n_before:]
        base = side(other) * half
        block_of = blocks_of(ids_ref, other, kt)
        for ref in (grad, curv)[n_before:]:
            ref[...] = jnp.zeros_like(ref)

        def add(p):
            tail = scaled_ref[p, count * columns :, :].astype(F32)
            for r in range(count):
                row_block = base + p * count + r
                weights = jnp.broadcast_to(tail[r : r + 1, :], (rows, rows)).T
                placed = [tiles_ref[row_block, k] for k in range(kt)]
                sums = jnp.dot(
                    scaled_ref[p, r * columns : (r + 1) * columns, :],
                    jnp.concatenate(placed, axis=1),
                    preferred_element_type=F32,
                )
                for k in range(kt):
                    block = block_of(p * count + r, k)
                    grad[block] += sums[:, k * width : (k + 1) * width]
                    wide = placed[k].astype(F32)
                    square = wide * wide * weights
                    curv[block] += jnp.sum(square.reshape(rows // 8, 8, width), axis=0)

        for p in range(sources):
            add(p)

        if other:

            @pl.loop(0, groups)
            def _(g):
                lines = []
                for b in range(owned):
                    at = g * owned + b
                    rounded = grad[at].astype(BF16)
                    out[0][g, b * columns : (b + 1) * columns, :] = rounded
                    if keep_error:
                        grad[at] -= rounded.astype(F32)
                    lines.append(jnp.sum(curv[at], axis=0, keepdims=True))
                lines.append(jnp.zeros((PAD - owned, width), F32))
                out[0][g, owned * columns :, :] = jnp.concatenate(lines, axis=0).astype(BF16)

    out_shape = [
        jax.ShapeDtypeStruct((local_blocks, columns, width), F32),
        jax.ShapeDtypeStruct((local_blocks, 8, width), F32),
    ]
    if other:
        out_shape.append(jax.ShapeDtypeStruct((groups, owned * columns + PAD, width), BF16))
    return pl.pallas_call(
        kernel,
        in_specs=whole(3 + n_before, 0),
        out_specs=whole(len(out_shape), 0),
        out_shape=out_shape,
        input_output_aliases={3 + i: i for i in range(n_before)},
        compiler_params=params(),
    )(ids, tiles, scaled, *before)


def update(parts, exact, known, copies, owned):
    sources, height, width = parts.shape
    columns = (height - PAD) // owned
    shape = (owned, columns, width)
    first = known is None

    def kernel(parts_ref, exact_ref, *refs):
        sent_ref = refs[-1]

        def total(lo, hi):
            value = parts_ref[0, lo:hi, :].astype(F32)
            for s in range(1, sources):
                value = value + parts_ref[s, lo:hi, :].astype(F32)
            return value

        curvature = total(owned * columns, height)
        for b in range(owned):
            gradient = total(b * columns, (b + 1) * columns)
            coef = exact_ref[b]
            new = coef + STEP_SIZE * (gradient - RIDGE * coef) / (curvature[b : b + 1] + RIDGE)
            if first:
                refs[0][b] = new
            else:
                new = new - refs[0][0, b].astype(F32)
            for c in range(copies):
                sent_ref[c, b] = new.astype(BF16)

    out_shape = [jax.ShapeDtypeStruct((copies,) + shape, BF16)]
    if first:
        out_shape.insert(0, jax.ShapeDtypeStruct(shape, F32))
    return pl.pallas_call(
        kernel,
        in_specs=whole(2 + (not first), 0),
        out_specs=whole(len(out_shape), 0),
        out_shape=out_shape,
        compiler_params=params(),
    )(parts, exact, *(() if first else (known,)))


def finish(known, change):
    blocks, columns, width = known.shape
    step = 16
    pieces = columns // step

    def kernel(known_ref, change_ref, out_hbm, held, sem):
        copies = []
        for p in range(pieces):
            at = pl.ds(p * step, step)
            for b in range(blocks):
                value = known_ref[b, at, :].astype(F32) + change_ref[b, at, :].astype(F32)
                held[at, b * width : (b + 1) * width] = value
            copies.append(pltpu.make_async_copy(held.at[at], out_hbm.at[at], sem.at[p]))
            copies[p].start()
        for copy in copies:
            copy.wait()

    shape = (columns, blocks * width)
    return pl.pallas_call(
        kernel,
        in_specs=whole(2, 0),
        out_specs=pl.BlockSpec(memory_space=pltpu.HBM),
        out_shape=jax.ShapeDtypeStruct(shape, F32),
        scratch_shapes=[pltpu.VMEM(shape, F32), pltpu.SemaphoreType.DMA((pieces,))],
        compiler_params=params(),
    )(known, change)


def make_body(n_row, n_feat):
    n_yz = n_feat // 2
    chips = [[2 * i + core for i in range(n_yz)] for core in range(2)]
    other_core = [(i, i ^ 1) for i in range(n_feat)]

    def swap_core(x):
        return lax.ppermute(x, "feat", other_core)

    def exchange_feat(x):
        return lax.all_to_all(x, "feat", 0, 0, axis_index_groups=chips, tiled=True)

    def exchange_row(x):
        return lax.all_to_all(x, "row", 0, 0, tiled=True)

    def body(design_tiles, block_ids, responses, live_groups, start_coef):
        row = lax.axis_index("row")
        feat = lax.axis_index("feat")
        _, owners, slots, kt, rows, width = design_tiles.shape
        row_blocks = owners * slots
        features, columns = start_coef.shape
        local_blocks = features // width
        tiles = design_tiles.reshape(row_blocks, kt, rows, width)
        resp_t = responses.reshape(row_blocks, rows, columns).swapaxes(1, 2)
        start_t = start_coef.T
        ids = lax.dynamic_index_in_dim(block_ids, row, 0, keepdims=False).reshape(-1)
        ids = (ids - feat * local_blocks).astype(jnp.int32).reshape(2, -1)
        ids = jnp.pad(ids, ((0, 0), (0, -ids.shape[1] % LANES)))
        share = row_blocks // n_feat
        owned = local_blocks // n_row

        sent, carried = None, ()
        for iteration in range(ITERS):
            ends = iteration == ITERS - 1
            if iteration == 0:
                ahead, known, exact = predict_first(ids, tiles, start_t, owned, BF16)
            else:
                ahead = predict_half(ids, tiles, known, True)
            arrived = swap_core(ahead)
            kept = predict_half(ids, tiles, known, False)
            pair = (kept + arrived.astype(F32)).astype(BF16)
            parts = exchange_feat(pair).reshape(n_yz, share, columns, rows)
            scaled = exchange_feat(weigh(n_feat, live_groups, parts, resp_t, n_yz))
            scaled_there = swap_core(scaled)
            before = gradient_half(
                ids, tiles, scaled, False, local_blocks, n_row, carried, False
            )
            error, _, partial = gradient_half(
                ids, tiles, scaled_there, True, local_blocks, n_row, before, not ends
            )
            carried = (error,)
            *new, sent = update(exchange_row(partial), exact, sent, n_row, owned)
            gathered = exchange_row(sent).reshape(local_blocks, columns, width)
            if ends:
                return finish(known, gathered).T
            known, exact = gathered, new[0]

    return body


def solution(mesh):
    in_specs = (
        P("row", None, None, "feat", None, None),
        P(None, None, None, "feat"),
        P("row", None, None, None, None),
        P(),
        P("feat", None),
    )
    return jax.shard_map(
        make_body(mesh.shape["row"], mesh.shape["feat"]),
        mesh=mesh,
        in_specs=in_specs,
        out_specs=P("feat", None),
        check_vma=False,
    )
```

```python
import jax
import jax.numpy as jnp
from jax import lax
from jax.experimental import pallas as pl
from jax.experimental.pallas import tpu as pltpu
from jax.sharding import PartitionSpec as P

ITERS = 2
STEP_SIZE = 0.25
RIDGE = 0.05
F32 = jnp.float32
BF16 = jnp.bfloat16
VMEM_LIMIT = 16 * 1024 * 1024
FIRST_LIMIT = 51 * 1024 * 1024

LANES = 128
PAD = 16


def params(limit=VMEM_LIMIT):
    return pltpu.CompilerParams(vmem_limit_bytes=limit)


def whole(count, scalars):
    smem = pl.BlockSpec(memory_space=pltpu.SMEM)
    vmem = pl.BlockSpec(memory_space=pltpu.VMEM)
    return [smem] * scalars + [vmem] * count


def place(n_feat):
    feat = lax.axis_index("feat")
    return lax.axis_index("row"), lax.rem(feat, 2), lax.div(feat, 2)


def side(other):
    core = lax.axis_index("feat") % 2
    return 1 - core if other else core


def blocks_of(ids_ref, other, kt):
    line = ids_ref[pl.ds(side(other), 1), :]
    return lambda row_block, k: line[0, row_block * kt + k]


def predict_pair(block_of, tiles_ref, coef_ref, out_ref, put, at, kt):
    picked, placed = [], []
    for r in range(2):
        picked.append(jnp.concatenate([coef_ref[block_of(put + r, k)] for k in range(kt)], axis=1))
        placed.append(jnp.concatenate([tiles_ref[at + r, k] for k in range(kt)], axis=1))
    both = lax.dot_general(
        jnp.concatenate(picked, axis=0),
        jnp.concatenate(placed, axis=0),
        (((1,), (1,)), ((), ())),
        preferred_element_type=F32,
    )
    columns, rows = picked[0].shape[0], placed[0].shape[0]
    out_ref[put] = both[:columns, :rows].astype(out_ref.dtype)
    out_ref[put + 1] = both[columns:, rows:].astype(out_ref.dtype)


def predict_first(ids, tiles, start_t, owned, dtype):
    row_blocks, kt, rows, width = tiles.shape
    columns, features = start_t.shape
    blocks = features // width
    half = row_blocks // 2
    step = 4
    pieces = half // step
    coef_pieces = 8
    share = features // coef_pieces

    def kernel(ids_vmem, tiles_hbm, start_hbm, out_ref, coef_ref, own_ref, *scratch):
        held, tile_sem, start_ref, start_sem, ids_ref, ids_sem = scratch
        other = side(True)
        base = other * half
        block_of = lambda row_block, k: ids_ref[other, row_block * kt + k]
        ids_copy = pltpu.make_async_copy(ids_vmem, ids_ref, ids_sem)
        starts, copies = [], []
        for p in range(coef_pieces):
            at = pl.ds(p * share, share)
            starts.append(
                pltpu.make_async_copy(start_hbm.at[:, at], start_ref.at[:, at], start_sem.at[p])
            )
        for p in range(pieces):
            copies.append(
                pltpu.make_async_copy(
                    tiles_hbm.at[pl.ds(base + p * step, step)],
                    held.at[pl.ds(p * step, step)],
                    tile_sem.at[p],
                )
            )
        for copy in starts + [ids_copy] + copies:
            copy.start()
        for p in range(coef_pieces):
            starts[p].wait()
            for b in range(p * blocks // coef_pieces, (p + 1) * blocks // coef_pieces):
                coef_ref[b] = start_ref[:, b * width : (b + 1) * width].astype(BF16)
        for b in range(owned):
            at = pl.multiple_of((lax.axis_index("row") * owned + b) * width, width)
            own_ref[b] = start_ref[:, pl.ds(at, width)]
        ids_copy.wait()
        for p in range(pieces):
            copies[p].wait()
            for r in range(0, step, 2):
                at = p * step + r
                predict_pair(block_of, held, coef_ref, out_ref, at, at, kt)

    hbm = pl.BlockSpec(memory_space=pltpu.HBM)
    return pl.pallas_call(
        kernel,
        in_specs=whole(1, 0) + [hbm, hbm],
        out_specs=whole(3, 0),
        out_shape=[
            jax.ShapeDtypeStruct((half, columns, rows), dtype),
            jax.ShapeDtypeStruct((blocks, columns, width), BF16),
            jax.ShapeDtypeStruct((owned, columns, width), F32),
        ],
        scratch_shapes=[
            pltpu.VMEM((half, kt, rows, width), BF16),
            pltpu.SemaphoreType.DMA((pieces,)),
            pltpu.VMEM(start_t.shape, F32),
            pltpu.SemaphoreType.DMA((coef_pieces,)),
            pltpu.SMEM(ids.shape, jnp.int32),
            pltpu.SemaphoreType.DMA(()),
        ],
        compiler_params=params(FIRST_LIMIT),
    )(ids, tiles, start_t)


def predict_half(ids, tiles, coef, other):
    row_blocks, kt, rows, width = tiles.shape
    columns = coef.shape[1]
    half = row_blocks // 2

    def kernel(ids_ref, tiles_ref, coef_ref, out_ref):
        base = side(other) * half
        block_of = blocks_of(ids_ref, other, kt)
        for r in range(0, half, 2):
            predict_pair(block_of, tiles_ref, coef_ref, out_ref, r, base + r, kt)

    return pl.pallas_call(
        kernel,
        in_specs=whole(3, 0),
        out_specs=whole(1, 0)[0],
        out_shape=jax.ShapeDtypeStruct((half, columns, rows), F32),
        compiler_params=params(),
    )(ids, tiles, coef)


def weigh(n_feat, live, parts, resp_t, copies):
    sources, count, columns, rows = parts.shape
    threshold = 1.4 * columns**0.5
    height = count * columns + PAD

    slots = resp_t.shape[0] // live.shape[1]

    def kernel(live_ref, parts_ref, resp_ref, out_ref):
        row, core, chip = place(n_feat)
        first = (core * (n_feat // 2) + chip) * count
        at = lax.broadcasted_iota(jnp.int32, live.shape, 0) == row
        at &= lax.broadcasted_iota(jnp.int32, live.shape, 1) == first // slots
        flag = jnp.sum(jnp.where(at, live_ref[...].astype(F32), 0.0), axis=0, keepdims=True)
        flag = jnp.sum(flag, axis=1, keepdims=True)
        lines = []
        for r in range(count):
            predicted = parts_ref[0, r].astype(F32)
            for s in range(1, sources):
                predicted = predicted + parts_ref[s, r].astype(F32)
            residual = resp_ref[first + r].astype(F32) - predicted
            norm = jnp.sqrt(jnp.sum(residual * residual, axis=0, keepdims=True))
            weight = flag * threshold / jnp.maximum(norm, threshold)
            scaled = (weight * residual).astype(BF16)
            for c in range(copies):
                out_ref[c, r * columns : (r + 1) * columns, :] = scaled
            lines.append(weight)
        lines.append(jnp.zeros((PAD - count, rows), F32))
        tail = jnp.concatenate(lines, axis=0).astype(BF16)
        for c in range(copies):
            out_ref[c, count * columns :, :] = tail

    return pl.pallas_call(
        kernel,
        in_specs=whole(3, 0),
        out_specs=whole(1, 0)[0],
        out_shape=jax.ShapeDtypeStruct((copies, height, rows), BF16),
        compiler_params=params(),
    )(live, parts, resp_t)


def gradient_half(ids, tiles, scaled, other, local_blocks, groups, before, keep_error):
    row_blocks, kt, rows, width = tiles.shape
    sources, height, _ = scaled.shape
    half = row_blocks // 2
    count = half // sources
    columns = (height - PAD) // count
    owned = local_blocks // groups
    n_before = len(before)

    def kernel(ids_ref, tiles_ref, scaled_ref, *refs):
        grad, curv, *out = refs[n_before:]
        base = side(other) * half
        block_of = blocks_of(ids_ref, other, kt)
        for ref in (grad, curv)[n_before:]:
            ref[...] = jnp.zeros_like(ref)

        def add(p):
            tail = scaled_ref[p, count * columns :, :].astype(F32)
            for r in range(count):
                row_block = base + p * count + r
                weights = jnp.broadcast_to(tail[r : r + 1, :], (rows, rows)).T
                placed = [tiles_ref[row_block, k] for k in range(kt)]
                sums = jnp.dot(
                    scaled_ref[p, r * columns : (r + 1) * columns, :],
                    jnp.concatenate(placed, axis=1),
                    preferred_element_type=F32,
                )
                for k in range(kt):
                    block = block_of(p * count + r, k)
                    grad[block] += sums[:, k * width : (k + 1) * width]
                    wide = placed[k].astype(F32)
                    square = wide * wide * weights
                    curv[block] += jnp.sum(square.reshape(rows // 8, 8, width), axis=0)

        for p in range(sources):
            add(p)

        if other:

            @pl.loop(0, groups)
            def _(g):
                lines = []
                for b in range(owned):
                    at = g * owned + b
                    rounded = grad[at].astype(BF16)
                    out[0][g, b * columns : (b + 1) * columns, :] = rounded
                    if keep_error:
                        grad[at] -= rounded.astype(F32)
                    lines.append(jnp.sum(curv[at], axis=0, keepdims=True))
                lines.append(jnp.zeros((PAD - owned, width), F32))
                out[0][g, owned * columns :, :] = jnp.concatenate(lines, axis=0).astype(BF16)

    out_shape = [
        jax.ShapeDtypeStruct((local_blocks, columns, width), F32),
        jax.ShapeDtypeStruct((local_blocks, 8, width), F32),
    ]
    if other:
        out_shape.append(jax.ShapeDtypeStruct((groups, owned * columns + PAD, width), BF16))
    return pl.pallas_call(
        kernel,
        in_specs=whole(3 + n_before, 0),
        out_specs=whole(len(out_shape), 0),
        out_shape=out_shape,
        input_output_aliases={3 + i: i for i in range(n_before)},
        compiler_params=params(),
    )(ids, tiles, scaled, *before)


def update(parts, exact, known, copies, owned):
    sources, height, width = parts.shape
    columns = (height - PAD) // owned
    shape = (owned, columns, width)
    first = known is None

    def kernel(parts_ref, exact_ref, *refs):
        sent_ref = refs[-1]

        def total(lo, hi):
            value = parts_ref[0, lo:hi, :].astype(F32)
            for s in range(1, sources):
                value = value + parts_ref[s, lo:hi, :].astype(F32)
            return value

        curvature = total(owned * columns, height)
        for b in range(owned):
            gradient = total(b * columns, (b + 1) * columns)
            coef = exact_ref[b]
            new = coef + STEP_SIZE * (gradient - RIDGE * coef) / (curvature[b : b + 1] + RIDGE)
            if first:
                refs[0][b] = new
            else:
                new = new - refs[0][0, b].astype(F32)
            for c in range(copies):
                sent_ref[c, b] = new.astype(BF16)

    out_shape = [jax.ShapeDtypeStruct((copies,) + shape, BF16)]
    if first:
        out_shape.insert(0, jax.ShapeDtypeStruct(shape, F32))
    return pl.pallas_call(
        kernel,
        in_specs=whole(2 + (not first), 0),
        out_specs=whole(len(out_shape), 0),
        out_shape=out_shape,
        compiler_params=params(),
    )(parts, exact, *(() if first else (known,)))


def finish(known, change):
    blocks, columns, width = known.shape
    step = 16
    pieces = columns // step

    def kernel(known_ref, change_ref, out_hbm, held, sem):
        copies = []
        for p in range(pieces):
            at = pl.ds(p * step, step)
            for b in range(blocks):
                value = known_ref[b, at, :].astype(F32) + change_ref[b, at, :].astype(F32)
                held[at, b * width : (b + 1) * width] = value
            copies.append(pltpu.make_async_copy(held.at[at], out_hbm.at[at], sem.at[p]))
            copies[p].start()
        for copy in copies:
            copy.wait()

    shape = (columns, blocks * width)
    return pl.pallas_call(
        kernel,
        in_specs=whole(2, 0),
        out_specs=pl.BlockSpec(memory_space=pltpu.HBM),
        out_shape=jax.ShapeDtypeStruct(shape, F32),
        scratch_shapes=[pltpu.VMEM(shape, F32), pltpu.SemaphoreType.DMA((pieces,))],
        compiler_params=params(),
    )(known, change)


def make_body(n_row, n_feat):
    n_yz = n_feat // 2
    chips = [[2 * i + core for i in range(n_yz)] for core in range(2)]
    other_core = [(i, i ^ 1) for i in range(n_feat)]

    def swap_core(x):
        return lax.ppermute(x, "feat", other_core)

    def exchange_feat(x):
        return lax.all_to_all(x, "feat", 0, 0, axis_index_groups=chips, tiled=True)

    def exchange_row(x):
        return lax.all_to_all(x, "row", 0, 0, tiled=True)

    def body(design_tiles, block_ids, responses, live_groups, start_coef):
        row = lax.axis_index("row")
        feat = lax.axis_index("feat")
        _, owners, slots, kt, rows, width = design_tiles.shape
        row_blocks = owners * slots
        features, columns = start_coef.shape
        local_blocks = features // width
        tiles = design_tiles.reshape(row_blocks, kt, rows, width)
        resp_t = responses.reshape(row_blocks, rows, columns).swapaxes(1, 2)
        start_t = start_coef.T
        ids = lax.dynamic_index_in_dim(block_ids, row, 0, keepdims=False).reshape(-1)
        ids = (ids - feat * local_blocks).astype(jnp.int32).reshape(2, -1)
        ids = jnp.pad(ids, ((0, 0), (0, -ids.shape[1] % LANES)))
        share = row_blocks // n_feat
        owned = local_blocks // n_row

        sent, carried = None, ()
        for iteration in range(ITERS):
            ends = iteration == ITERS - 1
            if iteration == 0:
                ahead, known, exact = predict_first(ids, tiles, start_t, owned, BF16)
            else:
                ahead = predict_half(ids, tiles, known, True)
            arrived = swap_core(ahead)
            kept = predict_half(ids, tiles, known, False)
            pair = (kept + arrived.astype(F32)).astype(BF16)
            parts = exchange_feat(pair).reshape(n_yz, share, columns, rows)
            scaled = exchange_feat(weigh(n_feat, live_groups, parts, resp_t, n_yz))
            scaled_there = swap_core(scaled)
            before = gradient_half(
                ids, tiles, scaled, False, local_blocks, n_row, carried, False
            )
            error, _, partial = gradient_half(
                ids, tiles, scaled_there, True, local_blocks, n_row, before, not ends
            )
            carried = (error,)
            *new, sent = update(exchange_row(partial), exact, sent, n_row, owned)
            gathered = exchange_row(sent).reshape(local_blocks, columns, width)
            if ends:
                return finish(known, gathered).T
            known, exact = gathered, new[0]

    return body


def solution(mesh):
    in_specs = (
        P("row", None, None, "feat", None, None),
        P(None, None, None, "feat"),
        P("row", None, None, None, None),
        P(),
        P("feat", None),
    )
    return jax.shard_map(
        make_body(mesh.shape["row"], mesh.shape["feat"]),
        mesh=mesh,
        in_specs=in_specs,
        out_specs=P("feat", None),
        check_vma=False,
    )
```
